128 devices in a mesh: ctx: 16 (over x, y_hi, core), head: 8 (over z, y_lo).
Axes of the slice: x: 4, y: 4 (y_hi: 2, y_lo: 2; y = y_hi * 2 + y_lo), z: 4, core: 2. Of those that a mesh axis runs over, the one named last changes fastest.
Arguments:
- hidden: bfloat16 [4096, 5120], P('ctx'), may hold values from -320 to 320
- positions: int32 [4096], replicated, may hold values from 0 to 4095, each once
- w_query: bfloat16 [5120, 5120], P(None, 'head'), may hold values from -0.078125 to 0.078125
- key_matrix: bfloat16 [5120, 1024], P(None, 'head'), may hold values from -0.15625 to 0.15625
- value_matrix: bfloat16 [5120, 1024], P(None, 'head'), may hold values from -0.078125 to 0.078125
- w_out: bfloat16 [5120, 5120], P('head'), may hold values from -0.3125 to 0.3125
- stored_keys: bfloat16 [24576, 1024], P('ctx', 'head'), may hold values from -33 to 33
- stored_values: bfloat16 [24576, 1024], P('ctx', 'head'), may hold values from -6 to 6
- kept_pages: int32 [8, 96], replicated, may hold values from 0 to 191, as said below
- page_slot: int32 [192], replicated, may hold values from 0 to 191, each once
Outputs:
- layer_out: float32 [4096, 5120], P('ctx', 'head')
The draws below stay inside these ranges and needn't reach their ends.
Inputs may be any that keep to these rules, and one draw needn't show every extreme that they name: Each row of kept_pages names 96 different logical pages, page 0 and page 192 - 1 among them. `positions`: every position 0 to 4095 occurs once. `page_slot`: every slot occurs once; slot s holds cache rows s * 128 to s * 128 + 127.
All inputs are finite; a program needn't handle non-finite values.
Results may differ from the reference program's by a relative error of at most 0.0076.
Values may be sent and summed in bfloat16 or wider, within the bound.
A program may use at most 384 MiB of HBM per device.

```python
import math
import jax
import jax.numpy as jnp
from jax import lax

MODEL_WIDTH = 5120
KEY_HEADS = 8
QUERY_GROUP = 5
HEAD_WIDTH = 128
PAGE = 128
TURN_TOKENS_LOCAL = 256
HQ = 40
TURN_TOKENS = 4096
PAGE_COUNT = 192
CACHED_TOKENS = 24576
KEPT_COUNT = 96
N_CTX = 16


def draw_hidden(key, part):
    key = jax.random.fold_in(key, 3)
    base_draw = jnp.clip(jax.random.normal(key, (TURN_TOKENS, MODEL_WIDTH), jnp.float32), -4.0, 4.0)
    return base_draw.astype(jnp.bfloat16)


def draw_stored_keys(key, part):
    key = jax.random.fold_in(key, 5)
    joined_shape = (CACHED_TOKENS, KEY_HEADS * HEAD_WIDTH)
    base_draw = 2.0 * jnp.clip(jax.random.normal(key, joined_shape, jnp.float32), -4.0, 4.0)
    return base_draw.astype(jnp.bfloat16)


def draw_kept_pages(key, part):
    key = jax.random.fold_in(key, 7)
    per_head_keys = jax.random.split(key, KEY_HEADS)
    page_ranks = jax.vmap(lambda single: jax.random.permutation(single, PAGE_COUNT))(per_head_keys).astype(jnp.int32)
    page_numbers = jnp.arange(PAGE_COUNT, dtype=jnp.int32)
    extra_bias = jnp.where((page_numbers == 0) | (page_numbers == PAGE_COUNT - 1), PAGE_COUNT, 0).astype(jnp.int32)
    unused_item, picked_pages = lax.top_k(page_ranks + extra_bias[None, :], KEPT_COUNT)
    return picked_pages.astype(jnp.int32)


def block_levels(key, shape, pieces, least, largest):
    gain, own = 1.0, jax.random.fold_in(key, 6)
    for position, parts in pieces:
        heights = jnp.exp(jax.random.uniform(jax.random.fold_in(own, position), (parts,), jnp.float32, least / len(pieces), largest / len(pieces)))
        gain = gain * jnp.repeat(heights, shape[position] // parts).reshape([-1 if axis == position else 1 for axis in range(len(shape))])
    return gain


def bell_draw(key, extent, spread, bound, cuts=(), kind=jnp.bfloat16):
    level = block_levels(key, extent, cuts, -0.22, 0.18) if cuts else 1.0
    entries = jax.random.normal(key, extent, jnp.float32) * spread * level
    return jnp.minimum(jnp.maximum(entries, -bound), bound).astype(kind)


def setup_inputs(seed: int = 0) -> dict:
    arg_keys = jax.random.split(jax.random.key(seed), 11)
    hidden = draw_hidden(jax.random.fold_in(arg_keys[10], 71), 0)
    positions = jax.random.permutation(arg_keys[1], TURN_TOKENS).astype(jnp.int32)
    w_query = bell_draw(arg_keys[2], (MODEL_WIDTH, HQ * HEAD_WIDTH), MODEL_WIDTH ** -0.5, 0.078125, ((1, 8),))
    key_matrix = bell_draw(arg_keys[3], (MODEL_WIDTH, KEY_HEADS * HEAD_WIDTH), (MODEL_WIDTH // 4) ** -0.5, 0.15625, ((1, 8),))
    value_matrix = bell_draw(arg_keys[4], (MODEL_WIDTH, KEY_HEADS * HEAD_WIDTH), MODEL_WIDTH ** -0.5, 0.078125, ((1, 8),))
    w_out = bell_draw(arg_keys[5], (HQ * HEAD_WIDTH, MODEL_WIDTH), (HQ * HEAD_WIDTH // 16) ** -0.5, 0.3125, ((0, 8),))
    stored_keys = draw_stored_keys(jax.random.fold_in(arg_keys[10], 71), 0)
    stored_values = bell_draw(arg_keys[7], (CACHED_TOKENS, KEY_HEADS * HEAD_WIDTH), 1.0, 6.0, ((0, 16), (1, 8)))
    kept_pages = draw_kept_pages(jax.random.fold_in(arg_keys[10], 71), 0)
    page_slot = jax.random.permutation(arg_keys[9], PAGE_COUNT).astype(jnp.int32)
    return dict(hidden=hidden, positions=positions, w_query=w_query, key_matrix=key_matrix, value_matrix=value_matrix, w_out=w_out, stored_keys=stored_keys, stored_values=stored_values, kept_pages=kept_pages, page_slot=page_slot)


masked_low = -1e+30

def temper(abs_pos, head_size):
    steps_num = ((abs_pos + 1) // 8192).astype(jnp.float32)
    return (jnp.log(steps_num + 1.0) * 0.1 + 1.0) / math.sqrt(head_size)

def keep_rows(kept_pages, page_slot, page_len):
    total_pages = page_slot.shape[0]
    page_numbers = jnp.arange(total_pages, dtype=jnp.int32)
    logical = jnp.any(kept_pages[:, :, None] == page_numbers[None, None, :], axis=1)
    onehot = page_slot[:, None] == page_numbers[None, :]
    physical = jnp.any(logical[:, :, None] & onehot[None], axis=1)
    return jnp.repeat(physical, page_len, axis=1)

def reference(hidden, positions, w_query, key_matrix, value_matrix, w_out, stored_keys, stored_values, kept_pages, page_slot):
    scaling = temper(positions + CACHED_TOKENS, HEAD_WIDTH)
    query_rows = (jnp.dot(hidden, w_query, preferred_element_type=jnp.float32) * scaling[:, None]).astype(jnp.bfloat16)
    query_rows = query_rows.reshape(N_CTX, TURN_TOKENS_LOCAL, KEY_HEADS, QUERY_GROUP, HEAD_WIDTH)
    turn_keys = jnp.dot(hidden, key_matrix, preferred_element_type=jnp.float32).astype(jnp.bfloat16).reshape(TURN_TOKENS, KEY_HEADS, HEAD_WIDTH)
    turn_values = jnp.dot(hidden, value_matrix, preferred_element_type=jnp.float32).astype(jnp.bfloat16).reshape(TURN_TOKENS, KEY_HEADS, HEAD_WIDTH)
    joined_keys = jnp.concatenate([stored_keys.reshape(CACHED_TOKENS, KEY_HEADS, HEAD_WIDTH), turn_keys], axis=0)
    joined_values = jnp.concatenate([stored_values.reshape(CACHED_TOKENS, KEY_HEADS, HEAD_WIDTH), turn_values], axis=0)
    row_keep = keep_rows(kept_pages, page_slot, PAGE)
    pos_blocks = positions.reshape(N_CTX, TURN_TOKENS_LOCAL)

    def single_head_attend(head_number):
        per_head_keys = joined_keys[:, head_number].astype(jnp.float32)
        head_values = joined_values[:, head_number].astype(jnp.float32)
        cache_keep = row_keep[head_number]

        def one_block(block_in):
            block_q, block_pos = block_in
            head_q = block_q[:, head_number].astype(jnp.float32)
            causal = positions[None, :] <= block_pos[:, None]
            allowed = jnp.concatenate([jnp.broadcast_to(cache_keep[None, :], (TURN_TOKENS_LOCAL, CACHED_TOKENS)), causal], axis=1)
            scores = jnp.einsum('rgd,sd->grs', head_q, per_head_keys)
            scores = jnp.where(allowed[None], scores, masked_low)
            row_peak = lax.optimization_barrier(jnp.max(scores, axis=-1, keepdims=True))
            weights = jnp.where(allowed[None], jnp.exp(scores - row_peak), 0.0)
            totals = lax.optimization_barrier(jnp.sum(weights, axis=-1))
            rounded = lax.optimization_barrier(weights.astype(jnp.bfloat16)).astype(jnp.float32)
            summed = jnp.einsum('grs,sd->grd', rounded, head_values)
            return (summed / totals[..., None]).astype(jnp.bfloat16)
        return lax.map(one_block, (query_rows, pos_blocks))
    head_outputs = lax.map(single_head_attend, jnp.arange(KEY_HEADS, dtype=jnp.int32))
    head_outputs = jnp.transpose(head_outputs, (1, 3, 0, 2, 4)).reshape(TURN_TOKENS, KEY_HEADS * QUERY_GROUP * HEAD_WIDTH)
    return jnp.dot(head_outputs, w_out, preferred_element_type=jnp.float32)
```

```python
import functools
import math

import jax
import jax.numpy as jnp
from jax import lax
from jax.experimental import pallas as pl
from jax.experimental.pallas import tpu as pltpu
from jax.sharding import PartitionSpec as P

G = 5
W = 128
PAGE = 128
LOW = -1e30
MASKED = -3e38
MESH = pl.DeviceIdType.MESH
F32 = jnp.float32
BF16 = jnp.bfloat16


def places(x_count):
    ctx = lax.axis_index("ctx")
    head = lax.axis_index("head")
    x, y_hi, core = ctx // 4, (ctx // 2) % 2, ctx % 2

    def at(dx=0, dy=0, dc=0):
        return (lax.rem(x + dx, x_count) * 2 + lax.rem(y_hi + dy, 2)) * 2 + lax.rem(core + dc, 2)

    return ctx, head, core, at


def gather_kernel(
    x_count,
    z_count,
    scale_base,
    positions_ref,
    hidden_ref,
    w_query_ref,
    w_key_ref,
    w_value_ref,
    w_out_ref,
    keys_ref,
    values_ref,
    all_keys,
    all_values,
    all_new,
    queries,
    w_slab,
    hidden_vmem,
    wq_vmem,
    wk_vmem,
    wv_vmem,
    acc_vmem,
    q_vmem,
    new_vmem,
    send_sem,
    recv_sem,
    load_sem,
    local_sem,
):
    ctx, head, core, at = places(x_count)
    z, y_lo = head // 2, head % 2
    tokens = hidden_ref.shape[0]
    half = w_out_ref.shape[0] // 2
    columns = w_slab.shape[2]
    depth = hidden_ref.shape[1]
    steps = load_sem.shape[0]
    cut = depth // steps

    right, left, far = at(dx=1), at(dx=x_count - 1), at(dx=2)
    sibling, y_peer = at(dc=1), at(dy=1)
    cross = (ctx // 4 * 2 + lax.rem((ctx // 2) % 2 + core, 2)) * 2 + core
    out_peers = []
    for dz in range(z_count):
        for dl in range(2):
            if dz or dl:
                other = lax.rem(z + dz, z_count) * 2 + lax.rem(y_lo + dl, 2)
                back = lax.rem(z + z_count - dz, z_count) * 2 + lax.rem(y_lo + dl, 2)
                out_peers.append((cross if dl else ctx, other, back))

    barrier = pltpu.get_barrier_semaphore()
    met = [(c, head) for c in (right, left, far, sibling, y_peer)]
    met += [(c, h) for c, h, _ in out_peers]
    for device in met:
        pl.semaphore_signal(barrier, inc=1, device_id=device, device_id_type=MESH)
    pl.semaphore_wait(barrier, len(met))

    counter = [0]

    def send(source, target, device):
        i = counter[0]
        counter[0] += 1
        copy = pltpu.make_async_remote_copy(
            src_ref=source,
            dst_ref=target,
            send_sem=send_sem.at[i],
            recv_sem=recv_sem.at[i],
            device_id=device,
            device_id_type=MESH,
        )
        copy.start()
        return copy

    near = []
    for mine, everyone in ((keys_ref, all_keys), (values_ref, all_values)):
        near.append(send(mine, everyone.at[2 * (x_count - 1)], (right, head)))
        near.append(send(mine, everyone.at[2], (left, head)))
    pair = [
        send(mine, everyone.at[1], (sibling, head))
        for mine, everyone in ((keys_ref, all_keys), (values_ref, all_values))
    ]
    loads = []
    for i in range(steps):
        rows = pl.ds(i * cut, cut)
        pieces = [
            pltpu.make_async_copy(hidden_ref.at[:, rows], hidden_vmem.at[:, rows], load_sem.at[i, 0]),
            pltpu.make_async_copy(w_query_ref.at[rows], wq_vmem.at[rows], load_sem.at[i, 1]),
            pltpu.make_async_copy(w_key_ref.at[rows], wk_vmem.at[rows], load_sem.at[i, 2]),
            pltpu.make_async_copy(w_value_ref.at[rows], wv_vmem.at[rows], load_sem.at[i, 3]),
        ]
        for piece in pieces:
            piece.start()
        loads.append(pieces)
    my_half = pl.ds(pl.multiple_of(core * half, half), half)
    slabs = []
    for c, h, back in out_peers:
        cols = pl.ds(pl.multiple_of(h * columns, columns), columns)
        copy = send(w_out_ref.at[my_half, cols], w_slab.at[head, my_half], (c, h))
        slabs.append((copy, back))
    my_cols = pl.ds(pl.multiple_of(head * columns, columns), columns)
    own = [
        pltpu.make_async_copy(keys_ref, all_keys.at[0], local_sem.at[0]),
        pltpu.make_async_copy(values_ref, all_values.at[0], local_sem.at[1]),
        pltpu.make_async_copy(w_out_ref.at[:, my_cols], w_slab.at[head], local_sem.at[2]),
    ]
    for copy in own:
        copy.start()

    q_cols = wq_vmem.shape[1]
    for i in range(steps):
        for piece in loads[i]:
            piece.wait()
        rows = slice(i * cut, (i + 1) * cut)
        part = hidden_vmem[:, rows]
        for w_ref, first, last in (
            (wq_vmem, 0, q_cols),
            (wk_vmem, q_cols, q_cols + W),
            (wv_vmem, q_cols + W, q_cols + 2 * W),
        ):
            product = jnp.dot(part, w_ref[rows, :], preferred_element_type=F32)
            if i:
                acc_vmem[:, first:last] += product
            else:
                acc_vmem[:, first:last] = product
    my_positions = positions_ref[pl.ds(ctx, 1), :]
    spread = jnp.broadcast_to(my_positions, (tokens, tokens))
    diagonal = lax.broadcasted_iota(jnp.int32, (tokens, tokens), 0) == lax.broadcasted_iota(
        jnp.int32, (tokens, tokens), 1
    )
    column = jnp.sum(jnp.where(diagonal, spread, 0).astype(F32), axis=1, keepdims=True)
    thousands = jnp.floor((column + (scale_base + 1.0)) * (1.0 / 8192.0))
    scaling = (jnp.log(thousands + 1.0) * 0.1 + 1.0) / math.sqrt(W)
    q_vmem[...] = (acc_vmem[:, :q_cols] * scaling).astype(BF16)
    new_vmem[...] = acc_vmem[:, q_cols:].astype(BF16)

    rows_own, rows_peer = pl.ds(0, tokens), pl.ds(tokens, tokens)
    ask = send(q_vmem, queries.at[rows_peer], (y_peer, head))
    fresh = [
        send(new_vmem, all_new.at[2 * (x_count - 1)], (right, head)),
        send(new_vmem, all_new.at[2], (left, head)),
        send(new_vmem, all_new.at[4], (far, head)),
    ]
    fresh_pair = [send(new_vmem, all_new.at[1], (sibling, head))]
    late = [
        pltpu.make_async_copy(q_vmem, queries.at[rows_own], local_sem.at[3]),
        pltpu.make_async_copy(new_vmem, all_new.at[0], local_sem.at[4]),
    ]
    for copy in late:
        copy.start()
    for copy, slot in zip(fresh, (2 * (x_count - 1), 2, 4)):
        copy.wait_recv()
        fresh_pair.append(send(all_new.at[slot], all_new.at[slot + 1], (sibling, head)))

    last = 2 * (x_count - 1)
    across = []
    for copy, everyone, slot in zip(
        near, (all_keys, all_keys, all_values, all_values), (last, 2, last, 2)
    ):
        copy.wait_recv()
        if everyone is all_keys and slot == last:
            across.append(send(all_keys.at[last], all_keys.at[4], (right, head)))
        if everyone is all_values and slot == 2:
            across.append(send(all_values.at[2], all_values.at[4], (left, head)))
        pair.append(send(everyone.at[slot], everyone.at[slot + 1], (sibling, head)))
    slab_pair = []
    for copy, back in slabs:
        copy.wait_recv()
        slab_pair.append(send(w_slab.at[back, my_half], w_slab.at[back, my_half], (sibling, head)))
    for copy, everyone in zip(across, (all_keys, all_values)):
        copy.wait_recv()
        pair.append(send(everyone.at[4], everyone.at[5], (sibling, head)))
    for copy in pair + fresh_pair + slab_pair + [ask]:
        copy.wait_recv()
    for copy in near + pair + fresh + fresh_pair + across + slab_pair + [ask]:
        copy.wait_send()
    for copy, _ in slabs:
        copy.wait_send()
    for copy in own + late:
        copy.wait()


def gather(positions, hidden, w_query, w_key, w_value, w_out, keys, values, x_count, z_count):
    rows = keys.shape[0]
    tokens, depth = hidden.shape
    q_cols = w_query.shape[1]
    columns = w_out.shape[1] // (2 * z_count)
    anywhere = pl.BlockSpec(memory_space=pl.ANY)
    steps = 5
    copies = 40
    return pl.pallas_call(
        functools.partial(gather_kernel, x_count, z_count, float(rows * x_count * 4)),
        out_shape=[
            jax.ShapeDtypeStruct((2 * x_count, rows, W), BF16),
            jax.ShapeDtypeStruct((2 * x_count, rows, W), BF16),
            jax.ShapeDtypeStruct((2 * x_count, tokens, 2 * W), BF16),
            jax.ShapeDtypeStruct((2 * tokens, q_cols), BF16),
            jax.ShapeDtypeStruct((2 * z_count, w_out.shape[0], columns), BF16),
        ],
        in_specs=[pl.BlockSpec(memory_space=pltpu.VMEM)] + [anywhere] * 7,
        out_specs=[anywhere] * 5,
        scratch_shapes=[
            pltpu.VMEM((tokens, depth), BF16),
            pltpu.VMEM((depth, q_cols), BF16),
            pltpu.VMEM((depth, W), BF16),
            pltpu.VMEM((depth, W), BF16),
            pltpu.VMEM((tokens, q_cols + 2 * W), F32),
            pltpu.VMEM((tokens, q_cols), BF16),
            pltpu.VMEM((tokens, 2 * W), BF16),
            pltpu.SemaphoreType.DMA((copies,)),
            pltpu.SemaphoreType.DMA((copies,)),
            pltpu.SemaphoreType.DMA((steps, 4)),
            pltpu.SemaphoreType.DMA((5,)),
        ],
        compiler_params=pltpu.CompilerParams(
            collective_id=0, has_side_effects=True, vmem_limit_bytes=40 * 2**20
        ),
    )(positions, hidden, w_query, w_key, w_value, w_out, keys, values)


def attend_kernel(
    x_count,
    kept_ref,
    slot_ref,
    place_ref,
    positions_ref,
    q_ref,
    k_ref,
    v_ref,
    new_ref,
    acc_ref,
    stats_ref,
    m_ref,
    l_ref,
    bias_ref,
    list_ref,
):
    ctx, head = place_ref[0], place_ref[1]
    x, y_hi, core = ctx // 4, (ctx // 2) % 2, ctx % 2
    kept_count = kept_ref.shape[1]
    per_device = slot_ref.shape[0] // (4 * x_count)
    rows = q_ref.shape[0]
    tokens = rows // 2
    step = 4

    def note(i, count):
        slot = slot_ref[kept_ref[head, i]]
        where = slot // per_device
        place = lax.rem(where // 4 - x + x_count, x_count) * 2 + lax.rem(where % 2 + core, 2)
        list_ref[count] = place * per_device + slot % per_device
        return count + jnp.where((where // 2) % 2 == y_hi, 1, 0)

    count = lax.fori_loop(0, kept_count, note, jnp.int32(0))
    for j in range(step):
        list_ref[count + j] = 0

    m_ref[...] = jnp.full_like(m_ref, LOW)
    l_ref[...] = jnp.zeros_like(l_ref)
    acc_ref[...] = jnp.zeros_like(acc_ref)

    def absorb(keys, values, bias):
        width = keys.shape[0] // W
        values = jnp.concatenate([values, jnp.ones_like(values)], axis=1)
        for g in range(G):
            q = q_ref[:, g * W : (g + 1) * W]
            s = lax.dot_general(q, keys, (((1,), (1,)), ((), ())), preferred_element_type=F32)
            if bias is not None:
                s = s + bias()
            m_old = m_ref[g]
            m_new = jnp.maximum(m_old, jnp.max(s, axis=1, keepdims=True))
            rescale = jnp.exp(m_old - m_new)
            p = jnp.exp(s - jnp.concatenate([m_new] * width, axis=1)).astype(BF16)
            summed = jnp.dot(p, values, preferred_element_type=F32)
            l_ref[g] = l_ref[g] * rescale + summed[:, W:]
            acc_ref[g] = acc_ref[g] * rescale + summed[:, :W]
            m_ref[g] = m_new

    def pages(first):
        ks, vs = [], []
        for j in range(step):
            here = pl.ds(pl.multiple_of(list_ref[first + j] * PAGE, PAGE), PAGE)
            ks.append(k_ref[here, :])
            vs.append(v_ref[here, :])
        return jnp.concatenate(ks, axis=0), jnp.concatenate(vs, axis=0)

    def full(i, _):
        keys, values = pages(i * step)
        absorb(keys, values, None)
        return 0

    lax.fori_loop(0, count // step, full, 0)

    @pl.when(count % step > 0)
    def _():
        first = count // step * step
        keys, values = pages(first)
        lane = lax.broadcasted_iota(jnp.int32, (1, step * PAGE), 1) // PAGE
        row = jnp.where(lane + first < count, 0.0, MASKED)
        absorb(keys, values, lambda: row)

    diagonal = lax.broadcasted_iota(jnp.int32, (tokens, tokens), 0) == lax.broadcasted_iota(
        jnp.int32, (tokens, tokens), 1
    )

    def positions_of(which):
        return positions_ref[pl.ds(which, 1), :]

    def as_column(row):
        spread = jnp.where(diagonal, jnp.broadcast_to(row, (tokens, tokens)), 0)
        return jnp.sum(spread.astype(F32), axis=1, keepdims=True)

    peer = (x * 2 + 1 - y_hi) * 2 + core
    mine = jnp.concatenate(
        [as_column(positions_of(ctx)), as_column(positions_of(peer))], axis=0
    )
    blocks = new_ref.shape[0] // tokens
    for b in range(blocks // 2):
        theirs = []
        for dc in range(2):
            source = (lax.rem(x + b, x_count) * 2 + y_hi) * 2 + lax.rem(core + dc, 2)
            theirs.append(positions_of(source).astype(F32))
        late = jnp.concatenate(theirs, axis=1) > mine
        bias_ref[...] = jnp.where(late, MASKED, 0.0)
        here = slice(2 * b * tokens, 2 * (b + 1) * tokens)
        absorb(new_ref[here, :W], new_ref[here, W:], lambda: bias_ref[...])

    lane = lax.broadcasted_iota(jnp.int32, (rows, W), 1)
    stats = jnp.zeros((rows, W), F32)
    for g in range(G):
        stats = jnp.where(lane == g, m_ref[g], stats)
        stats = jnp.where(lane == 8 + g, l_ref[g], stats)
    stats_ref[...] = stats


def attend(kept, slots, place, positions, queries, keys, values, new, x_count):
    rows = queries.shape[0]
    vmem = pl.BlockSpec(memory_space=pltpu.VMEM)
    smem = pl.BlockSpec(memory_space=pltpu.SMEM)
    work = rows * G * (keys.shape[0] // 2 + new.shape[0])
    return pl.pallas_call(
        functools.partial(attend_kernel, x_count),
        out_shape=[
            jax.ShapeDtypeStruct((G, rows, W), F32),
            jax.ShapeDtypeStruct((rows, W), F32),
        ],
        in_specs=[smem] * 3 + [vmem] * 5,
        out_specs=[vmem] * 2,
        scratch_shapes=[
            pltpu.VMEM((G, rows, W), F32),
            pltpu.VMEM((G, rows, W), F32),
            pltpu.VMEM((rows, rows), F32),
            pltpu.SMEM((kept.shape[1] + 8,), jnp.int32),
        ],
        compiler_params=pltpu.CompilerParams(vmem_limit_bytes=56 * 2**20),
        cost_estimate=pl.CostEstimate(
            flops=work * 4 * W, bytes_accessed=16 * 2**20, transcendentals=work
        ),
    )(kept, slots, place, positions, queries, keys, values, new)


def on_device(
    hidden,
    positions,
    w_query,
    key_matrix,
    value_matrix,
    w_out,
    stored_keys,
    stored_values,
    kept_pages,
    page_slot,
):
    tokens = hidden.shape[0]
    ctx_count, head_count = lax.axis_size("ctx"), lax.axis_size("head")
    x_count, z_count = ctx_count // 4, head_count // 2
    ctx, head = lax.axis_index("ctx"), lax.axis_index("head")
    table = positions.reshape(ctx_count, tokens)
    keys, values, new, queries, slab = gather(
        table, hidden, w_query, key_matrix, value_matrix, w_out, stored_keys, stored_values,
        x_count, z_count,
    )
    place = jnp.stack([ctx, head]).astype(jnp.int32)
    acc, stats = attend(
        kept_pages, page_slot, place, table, queries, keys.reshape(-1, W), values.reshape(-1, W),
        new.reshape(-1, 2 * W), x_count,
    )
    swap = [(i, i ^ 2) for i in range(ctx_count)]
    acc_in = lax.ppermute(acc[:, tokens:], "ctx", swap)
    stats_in = lax.ppermute(stats[tokens:], "ctx", swap)
    mine, theirs = stats[:tokens], stats_in
    heads = []
    for g in range(G):
        m1, m2 = mine[:, g : g + 1], theirs[:, g : g + 1]
        l1, l2 = mine[:, 8 + g : 9 + g], theirs[:, 8 + g : 9 + g]
        m = jnp.maximum(m1, m2)
        a1, a2 = jnp.exp(m1 - m), jnp.exp(m2 - m)
        total = l1 * a1 + l2 * a2
        heads.append((acc[g, :tokens] * (a1 / total) + acc_in[g] * (a2 / total)).astype(BF16))
    heads = jnp.concatenate(heads, axis=1)
    everyone = lax.all_gather(heads, "head", axis=1, tiled=True)
    return jnp.dot(everyone, slab.reshape(-1, slab.shape[2]), preferred_element_type=F32)


def solution(mesh):
    placed = (
        P("ctx", None),
        P(),
        P(None, "head"),
        P(None, "head"),
        P(None, "head"),
        P("head", None),
        P("ctx", "head"),
        P("ctx", "head"),
        P(),
        P(),
    )
    return jax.shard_map(
        on_device, mesh=mesh, in_specs=placed, out_specs=P("ctx", "head"), check_vma=False
    )
```

```python
import functools
import math

import jax
import jax.numpy as jnp
from jax import lax
from jax.experimental import pallas as pl
from jax.experimental.pallas import tpu as pltpu
from jax.sharding import PartitionSpec as P

G = 5
W = 128
PAGE = 128
LOW = -1e30
MASKED = -3e38
MESH = pl.DeviceIdType.MESH
F32 = jnp.float32
BF16 = jnp.bfloat16


def places(x_count):
    ctx = lax.axis_index("ctx")
    head = lax.axis_index("head")
    x, y_hi, core = ctx // 4, (ctx // 2) % 2, ctx % 2

    def at(dx=0, dy=0, dc=0):
        return (lax.rem(x + dx, x_count) * 2 + lax.rem(y_hi + dy, 2)) * 2 + lax.rem(core + dc, 2)

    return ctx, head, core, at


def gather_kernel(
    x_count,
    z_count,
    scale_base,
    positions_ref,
    hidden_ref,
    w_query_ref,
    w_key_ref,
    w_value_ref,
    w_out_ref,
    keys_ref,
    values_ref,
    all_keys,
    all_values,
    all_new,
    queries,
    w_slab,
    hidden_vmem,
    wq_vmem,
    wk_vmem,
    wv_vmem,
    acc_vmem,
    q_vmem,
    new_vmem,
    send_sem,
    recv_sem,
    load_sem,
    local_sem,
):
    ctx, head, core, at = places(x_count)
    z, y_lo = head // 2, head % 2
    tokens = hidden_ref.shape[0]
    half = w_out_ref.shape[0] // 2
    columns = w_slab.shape[2]
    depth = hidden_ref.shape[1]
    steps = load_sem.shape[0]
    cut = depth // steps

    right, left, far = at(dx=1), at(dx=x_count - 1), at(dx=2)
    sibling, y_peer = at(dc=1), at(dy=1)
    cross = (ctx // 4 * 2 + lax.rem((ctx // 2) % 2 + core, 2)) * 2 + core
    out_peers = []
    for dz in range(z_count):
        for dl in range(2):
            if dz or dl:
                other = lax.rem(z + dz, z_count) * 2 + lax.rem(y_lo + dl, 2)
                back = lax.rem(z + z_count - dz, z_count) * 2 + lax.rem(y_lo + dl, 2)
                out_peers.append((cross if dl else ctx, other, back))

    barrier = pltpu.get_barrier_semaphore()
    met = [(c, head) for c in (right, left, far, sibling, y_peer)]
    met += [(c, h) for c, h, _ in out_peers]
    for device in met:
        pl.semaphore_signal(barrier, inc=1, device_id=device, device_id_type=MESH)
    pl.semaphore_wait(barrier, len(met))

    counter = [0]

    def send(source, target, device):
        i = counter[0]
        counter[0] += 1
        copy = pltpu.make_async_remote_copy(
            src_ref=source,
            dst_ref=target,
            send_sem=send_sem.at[i],
            recv_sem=recv_sem.at[i],
            device_id=device,
            device_id_type=MESH,
        )
        copy.start()
        return copy

    near = []
    for mine, everyone in ((keys_ref, all_keys), (values_ref, all_values)):
        near.append(send(mine, everyone.at[2 * (x_count - 1)], (right, head)))
        near.append(send(mine, everyone.at[2], (left, head)))
    pair = [
        send(mine, everyone.at[1], (sibling, head))
        for mine, everyone in ((keys_ref, all_keys), (values_ref, all_values))
    ]
    loads = []
    for i in range(steps):
        rows = pl.ds(i * cut, cut)
        pieces = [
            pltpu.make_async_copy(hidden_ref.at[:, rows], hidden_vmem.at[:, rows], load_sem.at[i, 0]),
            pltpu.make_async_copy(w_query_ref.at[rows], wq_vmem.at[rows], load_sem.at[i, 1]),
            pltpu.make_async_copy(w_key_ref.at[rows], wk_vmem.at[rows], load_sem.at[i, 2]),
            pltpu.make_async_copy(w_value_ref.at[rows], wv_vmem.at[rows], load_sem.at[i, 3]),
        ]
        for piece in pieces:
            piece.start()
        loads.append(pieces)
    my_half = pl.ds(pl.multiple_of(core * half, half), half)
    slabs = []
    for c, h, back in out_peers:
        cols = pl.ds(pl.multiple_of(h * columns, columns), columns)
        copy = send(w_out_ref.at[my_half, cols], w_slab.at[head, my_half], (c, h))
        slabs.append((copy, back))
    my_cols = pl.ds(pl.multiple_of(head * columns, columns), columns)
    own = [
        pltpu.make_async_copy(keys_ref, all_keys.at[0], local_sem.at[0]),
        pltpu.make_async_copy(values_ref, all_values.at[0], local_sem.at[1]),
        pltpu.make_async_copy(w_out_ref.at[:, my_cols], w_slab.at[head], local_sem.at[2]),
    ]
    for copy in own:
        copy.start()

    q_cols = wq_vmem.shape[1]
    for i in range(steps):
        for piece in loads[i]:
            piece.wait()
        rows = slice(i * cut, (i + 1) * cut)
        part = hidden_vmem[:, rows]
        for w_ref, first, last in (
            (wq_vmem, 0, q_cols),
            (wk_vmem, q_cols, q_cols + W),
            (wv_vmem, q_cols + W, q_cols + 2 * W),
        ):
            product = jnp.dot(part, w_ref[rows, :], preferred_element_type=F32)
            if i:
                acc_vmem[:, first:last] += product
            else:
                acc_vmem[:, first:last] = product
    my_positions = positions_ref[pl.ds(ctx, 1), :]
    spread = jnp.broadcast_to(my_positions, (tokens, tokens))
    diagonal = lax.broadcasted_iota(jnp.int32, (tokens, tokens), 0) == lax.broadcasted_iota(
        jnp.int32, (tokens, tokens), 1
    )
    column = jnp.sum(jnp.where(diagonal, spread, 0).astype(F32), axis=1, keepdims=True)
    thousands = jnp.floor((column + (scale_base + 1.0)) * (1.0 / 8192.0))
    scaling = (jnp.log(thousands + 1.0) * 0.1 + 1.0) / math.sqrt(W)
    q_vmem[...] = (acc_vmem[:, :q_cols] * scaling).astype(BF16)
    new_vmem[...] = acc_vmem[:, q_cols:].astype(BF16)

    rows_own, rows_peer = pl.ds(0, tokens), pl.ds(tokens, tokens)
    ask = send(q_vmem, queries.at[rows_peer], (y_peer, head))
    fresh = [
        send(new_vmem, all_new.at[2 * (x_count - 1)], (right, head)),
        send(new_vmem, all_new.at[2], (left, head)),
        send(new_vmem, all_new.at[4], (far, head)),
    ]
    fresh_pair = [send(new_vmem, all_new.at[1], (sibling, head))]
    late = [
        pltpu.make_async_copy(q_vmem, queries.at[rows_own], local_sem.at[3]),
        pltpu.make_async_copy(new_vmem, all_new.at[0], local_sem.at[4]),
    ]
    for copy in late:
        copy.start()
    for copy, slot in zip(fresh, (2 * (x_count - 1), 2, 4)):
        copy.wait_recv()
        fresh_pair.append(send(all_new.at[slot], all_new.at[slot + 1], (sibling, head)))

    last = 2 * (x_count - 1)
    across = []
    for copy, everyone, slot in zip(
        near, (all_keys, all_keys, all_values, all_values), (last, 2, last, 2)
    ):
        copy.wait_recv()
        if everyone is all_keys and slot == last:
            across.append(send(all_keys.at[last], all_keys.at[4], (right, head)))
        if everyone is all_values and slot == 2:
            across.append(send(all_values.at[2], all_values.at[4], (left, head)))
        pair.append(send(everyone.at[slot], everyone.at[slot + 1], (sibling, head)))
    slab_pair = []
    for copy, back in slabs:
        copy.wait_recv()
        slab_pair.append(send(w_slab.at[back, my_half], w_slab.at[back, my_half], (sibling, head)))
    for copy, everyone in zip(across, (all_keys, all_values)):
        copy.wait_recv()
        pair.append(send(everyone.at[4], everyone.at[5], (sibling, head)))
    for copy in pair + fresh_pair + slab_pair + [ask]:
        copy.wait_recv()
    for copy in near + pair + fresh + fresh_pair + across + slab_pair + [ask]:
        copy.wait_send()
    for copy, _ in slabs:
        copy.wait_send()
    for copy in own + late:
        copy.wait()


def gather(positions, hidden, w_query, w_key, w_value, w_out, keys, values, x_count, z_count):
    rows = keys.shape[0]
    tokens, depth = hidden.shape
    q_cols = w_query.shape[1]
    columns = w_out.shape[1] // (2 * z_count)
    anywhere = pl.BlockSpec(memory_space=pl.ANY)
    steps = 5
    copies = 40
    return pl.pallas_call(
        functools.partial(gather_kernel, x_count, z_count, float(rows * x_count * 4)),
        out_shape=[
            jax.ShapeDtypeStruct((2 * x_count, rows, W), BF16),
            jax.ShapeDtypeStruct((2 * x_count, rows, W), BF16),
            jax.ShapeDtypeStruct((2 * x_count, tokens, 2 * W), BF16),
            jax.ShapeDtypeStruct((2 * tokens, q_cols), BF16),
            jax.ShapeDtypeStruct((2 * z_count, w_out.shape[0], columns), BF16),
        ],
        in_specs=[pl.BlockSpec(memory_space=pltpu.VMEM)] + [anywhere] * 7,
        out_specs=[anywhere] * 5,
        scratch_shapes=[
            pltpu.VMEM((tokens, depth), BF16),
            pltpu.VMEM((depth, q_cols), BF16),
            pltpu.VMEM((depth, W), BF16),
            pltpu.VMEM((depth, W), BF16),
            pltpu.VMEM((tokens, q_cols + 2 * W), F32),
            pltpu.VMEM((tokens, q_cols), BF16),
            pltpu.VMEM((tokens, 2 * W), BF16),
            pltpu.SemaphoreType.DMA((copies,)),
            pltpu.SemaphoreType.DMA((copies,)),
            pltpu.SemaphoreType.DMA((steps, 4)),
            pltpu.SemaphoreType.DMA((5,)),
        ],
        compiler_params=pltpu.CompilerParams(
            collective_id=0, has_side_effects=True, vmem_limit_bytes=60 * 2**20
        ),
    )(positions, hidden, w_query, w_key, w_value, w_out, keys, values)


def attend_kernel(
    x_count,
    kept_ref,
    slot_ref,
    place_ref,
    positions_ref,
    q_ref,
    k_ref,
    v_ref,
    new_ref,
    acc_ref,
    stats_ref,
    m_ref,
    l_ref,
    bias_ref,
    list_ref,
):
    ctx, head = place_ref[0], place_ref[1]
    x, y_hi, core = ctx // 4, (ctx // 2) % 2, ctx % 2
    kept_count = kept_ref.shape[1]
    per_device = slot_ref.shape[0] // (4 * x_count)
    rows = q_ref.shape[0]
    tokens = rows // 2
    step = 4

    def note(i, count):
        slot = slot_ref[kept_ref[head, i]]
        where = slot // per_device
        place = lax.rem(where // 4 - x + x_count, x_count) * 2 + lax.rem(where % 2 + core, 2)
        list_ref[count] = place * per_device + slot % per_device
        return count + jnp.where((where // 2) % 2 == y_hi, 1, 0)

    count = lax.fori_loop(0, kept_count, note, jnp.int32(0))
    for j in range(step):
        list_ref[count + j] = 0

    m_ref[...] = jnp.full_like(m_ref, LOW)
    l_ref[...] = jnp.zeros_like(l_ref)
    acc_ref[...] = jnp.zeros_like(acc_ref)

    def absorb(keys, values, bias):
        width = keys.shape[0] // W
        for g in range(G):
            q = q_ref[:, g * W : (g + 1) * W]
            s = lax.dot_general(q, keys, (((1,), (1,)), ((), ())), preferred_element_type=F32)
            if bias is not None:
                s = s + bias()
            m_old = m_ref[g]
            m_new = jnp.maximum(m_old, jnp.max(s, axis=1, keepdims=True))
            rescale = jnp.exp(m_old - m_new)
            p = jnp.exp(s - jnp.concatenate([m_new] * width, axis=1))
            sums = sum(p[:, c * W : (c + 1) * W] for c in range(width))
            l_ref[g] = l_ref[g] * rescale + sums
            acc_ref[g] = acc_ref[g] * rescale + jnp.dot(
                p.astype(BF16), values, preferred_element_type=F32
            )
            m_ref[g] = m_new

    def pages(first, many):
        ks, vs = [], []
        for j in range(many):
            here = pl.ds(pl.multiple_of(list_ref[first + j] * PAGE, PAGE), PAGE)
            ks.append(k_ref[here, :])
            vs.append(v_ref[here, :])
        return jnp.concatenate(ks, axis=0), jnp.concatenate(vs, axis=0)

    def full(i, _):
        absorb(*pages(i * 2 * step, 2 * step), None)
        return 0

    lax.fori_loop(0, count // (2 * step), full, 0)

    @pl.when(count % (2 * step) >= step)
    def _():
        absorb(*pages(count // (2 * step) * (2 * step), step), None)

    @pl.when(count % step > 0)
    def _():
        first = count // step * step
        keys, values = pages(first, step)
        lane = lax.broadcasted_iota(jnp.int32, (1, step * PAGE), 1) // PAGE
        row = jnp.where(lane + first < count, 0.0, MASKED)
        absorb(keys, values, lambda: row)

    diagonal = lax.broadcasted_iota(jnp.int32, (tokens, tokens), 0) == lax.broadcasted_iota(
        jnp.int32, (tokens, tokens), 1
    )

    def positions_of(which):
        return positions_ref[pl.ds(which, 1), :]

    def as_column(row):
        spread = jnp.where(diagonal, jnp.broadcast_to(row, (tokens, tokens)), 0)
        return jnp.sum(spread.astype(F32), axis=1, keepdims=True)

    peer = (x * 2 + 1 - y_hi) * 2 + core
    mine = jnp.concatenate(
        [as_column(positions_of(ctx)), as_column(positions_of(peer))], axis=0
    )
    blocks = new_ref.shape[0] // tokens
    for b in range(blocks // 2):
        theirs = []
        for dc in range(2):
            source = (lax.rem(x + b, x_count) * 2 + y_hi) * 2 + lax.rem(core + dc, 2)
            theirs.append(positions_of(source).astype(F32))
        late = jnp.concatenate(theirs, axis=1) > mine
        bias_ref[...] = jnp.where(late, MASKED, 0.0)
        here = slice(2 * b * tokens, 2 * (b + 1) * tokens)
        absorb(new_ref[here, :W], new_ref[here, W:], lambda: bias_ref[...])

    lane = lax.broadcasted_iota(jnp.int32, (rows, W), 1)
    stats = jnp.zeros((rows, W), F32)
    for g in range(G):
        stats = jnp.where(lane == g, m_ref[g], stats)
        stats = jnp.where(lane == 8 + g, jnp.sum(l_ref[g], axis=1, keepdims=True), stats)
    stats_ref[...] = stats


def attend(kept, slots, place, positions, queries, keys, values, new, x_count):
    rows = queries.shape[0]
    vmem = pl.BlockSpec(memory_space=pltpu.VMEM)
    smem = pl.BlockSpec(memory_space=pltpu.SMEM)
    work = rows * G * (keys.shape[0] // 2 + new.shape[0])
    return pl.pallas_call(
        functools.partial(attend_kernel, x_count),
        out_shape=[
            jax.ShapeDtypeStruct((G, rows, W), F32),
            jax.ShapeDtypeStruct((rows, W), F32),
        ],
        in_specs=[smem] * 3 + [vmem] * 5,
        out_specs=[vmem] * 2,
        scratch_shapes=[
            pltpu.VMEM((G, rows, W), F32),
            pltpu.VMEM((G, rows, W), F32),
            pltpu.VMEM((rows, rows), F32),
            pltpu.SMEM((kept.shape[1] + 8,), jnp.int32),
        ],
        compiler_params=pltpu.CompilerParams(vmem_limit_bytes=60 * 2**20),
        cost_estimate=pl.CostEstimate(
            flops=work * 4 * W, bytes_accessed=16 * 2**20, transcendentals=work
        ),
    )(kept, slots, place, positions, queries, keys, values, new)


def finish_kernel(
    x_count,
    z_count,
    acc_ref,
    stats_ref,
    slab_ref,
    out_ref,
    acc_own,
    acc_in,
    stats_own,
    stats_in,
    slab_vmem,
    heads,
    send_sem,
    recv_sem,
    load_sem,
):
    ctx, head, core, at = places(x_count)
    z, y_lo = head // 2, head % 2
    tokens = stats_own.shape[0]
    y_peer = at(dy=1)

    def head_at(dz, dl):
        return lax.rem(z + dz, z_count) * 2 + lax.rem(y_lo + dl, 2)

    above, below, beside = head_at(1, 0), head_at(z_count - 1, 0), head_at(0, 1)
    barrier = pltpu.get_barrier_semaphore()
    met = [(y_peer, head), (ctx, above), (ctx, below), (ctx, beside)]
    for device in met:
        pl.semaphore_signal(barrier, inc=1, device_id=device, device_id_type=MESH)
    pl.semaphore_wait(barrier, len(met))

    counter = [0]
    started = []

    def send(source, target, device):
        i = counter[0]
        counter[0] += 1
        copy = pltpu.make_async_remote_copy(
            src_ref=source,
            dst_ref=target,
            send_sem=send_sem.at[i],
            recv_sem=recv_sem.at[i],
            device_id=device,
            device_id_type=MESH,
        )
        copy.start()
        started.append(copy)
        return copy

    rows_own, rows_peer = pl.ds(0, tokens), pl.ds(tokens, tokens)
    stats_copy = send(stats_ref.at[rows_peer], stats_in, (y_peer, head))
    parts = [send(acc_ref.at[g, rows_peer], acc_in.at[g], (y_peer, head)) for g in range(G)]
    loads = [
        pltpu.make_async_copy(stats_ref.at[rows_own], stats_own, load_sem.at[0]),
        pltpu.make_async_copy(acc_ref.at[:, rows_own], acc_own, load_sem.at[1]),
        pltpu.make_async_copy(slab_ref, slab_vmem, load_sem.at[2]),
    ]
    for load in loads:
        load.start()
    loads[0].wait()
    loads[1].wait()
    stats_copy.wait_recv()
    m1, m2 = stats_own[:, 0:8], stats_in[:, 0:8]
    l1, l2 = stats_own[:, 8:16], stats_in[:, 8:16]
    m = jnp.maximum(m1, m2)
    a1, a2 = jnp.exp(m1 - m), jnp.exp(m2 - m)
    total = l1 * a1 + l2 * a2

    def pass_on(who, g, device):
        return send(heads.at[who, g], heads.at[who, g], (ctx, device))

    first = [True]

    def use_first(who, g):
        if first[0]:
            loads[2].wait()
        use_now(who, g)

    def use_now(who, g):
        product = jnp.dot(
            heads[who, g], slab_vmem[who, g * W : (g + 1) * W, :], preferred_element_type=F32
        )
        if first[0]:
            out_ref[...] = product
            first[0] = False
        else:
            out_ref[...] += product

    up, down, side, up_side, down_side, two, two_side = ({} for _ in range(7))
    for t in range(G + 3):
        g = t
        if g < G:
            parts[g].wait_recv()
            weight1 = a1[:, g : g + 1] / total[:, g : g + 1]
            weight2 = a2[:, g : g + 1] / total[:, g : g + 1]
            heads[head, g] = (acc_own[g] * weight1 + acc_in[g] * weight2).astype(BF16)
            side[g] = pass_on(head, g, beside)
            up[g] = pass_on(head, g, above)
            down[g] = pass_on(head, g, below)
            use_first(head, g)
        g = t - 1
        if 0 <= g < G:
            side[g].wait_recv()
            up_side[g] = pass_on(beside, g, above)
            down_side[g] = pass_on(beside, g, below)
            up[g].wait_recv()
            down[g].wait_recv()
            if g % 2 == 0:
                two[g] = pass_on(below, g, above)
            else:
                two[g] = pass_on(above, g, below)
            use_now(beside, g)
            use_now(below, g)
            use_now(above, g)
        g = t - 2
        if 0 <= g < G:
            up_side[g].wait_recv()
            down_side[g].wait_recv()
            if g % 2 == 1:
                two_side[g] = pass_on(head_at(z_count - 1, 1), g, above)
            else:
                two_side[g] = pass_on(head_at(1, 1), g, below)
            use_now(head_at(z_count - 1, 1), g)
            use_now(head_at(1, 1), g)
        g = t - 3
        if 0 <= g < G:
            two[g].wait_recv()
            use_now(head_at(2, 0), g)
            two_side[g].wait_recv()
            use_now(head_at(2, 1), g)
    for copy in started:
        copy.wait_send()


def finish(acc, stats, slab, x_count, z_count):
    tokens = stats.shape[0] // 2
    anywhere = pl.BlockSpec(memory_space=pl.ANY)
    copies = 1 + G * 8
    return pl.pallas_call(
        functools.partial(finish_kernel, x_count, z_count),
        out_shape=jax.ShapeDtypeStruct((tokens, slab.shape[2]), F32),
        in_specs=[anywhere] * 3,
        out_specs=pl.BlockSpec(memory_space=pltpu.VMEM),
        scratch_shapes=[
            pltpu.VMEM((G, tokens, W), F32),
            pltpu.VMEM((G, tokens, W), F32),
            pltpu.VMEM((tokens, W), F32),
            pltpu.VMEM((tokens, W), F32),
            pltpu.VMEM(slab.shape, BF16),
            pltpu.VMEM((2 * z_count, G, tokens, W), BF16),
            pltpu.SemaphoreType.DMA((copies,)),
            pltpu.SemaphoreType.DMA((copies,)),
            pltpu.SemaphoreType.DMA((3,)),
        ],
        compiler_params=pltpu.CompilerParams(
            collective_id=1, has_side_effects=True, vmem_limit_bytes=60 * 2**20
        ),
    )(acc, stats, slab)


def on_device(
    hidden,
    positions,
    w_query,
    key_matrix,
    value_matrix,
    w_out,
    stored_keys,
    stored_values,
    kept_pages,
    page_slot,
):
    tokens = hidden.shape[0]
    ctx_count, head_count = lax.axis_size("ctx"), lax.axis_size("head")
    x_count, z_count = ctx_count // 4, head_count // 2
    ctx, head = lax.axis_index("ctx"), lax.axis_index("head")
    table = positions.reshape(ctx_count, tokens)
    keys, values, new, queries, slab = gather(
        table, hidden, w_query, key_matrix, value_matrix, w_out, stored_keys, stored_values,
        x_count, z_count,
    )
    place = jnp.stack([ctx, head]).astype(jnp.int32)
    acc, stats = attend(
        kept_pages, page_slot, place, table, queries, keys.reshape(-1, W), values.reshape(-1, W),
        new.reshape(-1, 2 * W), x_count,
    )
    return finish(acc, stats, slab, x_count, z_count)


def solution(mesh):
    placed = (
        P("ctx", None),
        P(),
        P(None, "head"),
        P(None, "head"),
        P(None, "head"),
        P("head", None),
        P("ctx", "head"),
        P("ctx", "head"),
        P(),
        P(),
    )
    return jax.shard_map(
        on_device, mesh=mesh, in_specs=placed, out_specs=P("ctx", "head"), check_vma=False
    )
```

```python
import functools
import math

import jax
import jax.numpy as jnp
from jax import lax
from jax.experimental import pallas as pl
from jax.experimental.pallas import tpu as pltpu
from jax.sharding import PartitionSpec as P

G = 5
W = 128
PAGE = 128
LOW = -1e30
MASKED = -3e38
BLOCK = 12
NEAR = 12
SIDE = 12
REST = 36
LIST = 128
PIECES = 3
MESH = pl.DeviceIdType.MESH
F32 = jnp.float32
BF16 = jnp.bfloat16


def places(x_count):
    ctx = lax.axis_index("ctx")
    head = lax.axis_index("head")
    x, y_hi, core = ctx // 4, (ctx // 2) % 2, ctx % 2

    def at(dx=0, dy=0, dc=0):
        return (lax.rem(x + dx, x_count) * 2 + lax.rem(y_hi + dy, 2)) * 2 + lax.rem(core + dc, 2)

    return ctx, head, core, at


def list_kernel(x_count, kept_ref, slot_ref, place_ref, list_ref):
    ctx, head = place_ref[0], place_ref[1]
    x, y_hi, core = ctx // 4, (ctx // 2) % 2, ctx % 2
    per_device = slot_ref.shape[0] // (4 * x_count)

    def clear(i, _):
        list_ref[i] = 0
        return 0

    lax.fori_loop(0, 4 * LIST, clear, 0, unroll=16)

    def note(i, counts):
        near, side, rest = counts
        slot = slot_ref[kept_ref[head, i]]
        where = slot // per_device
        dx = lax.rem(where // 4 - x + x_count, x_count)
        place = dx * 2 + lax.rem(where % 2 + core, 2)
        ours = (where // 2) % 2 == y_hi
        to_near = ours & (dx == 0) & (near < NEAR)
        to_side = ours & ((dx == 1) | (dx == x_count - 1)) & (side < SIDE)
        to_rest = ours & jnp.logical_not(to_near | to_side)
        spot = jnp.where(
            to_near, near, jnp.where(to_side, LIST + side, jnp.where(to_rest, 2 * LIST + rest, 4 * LIST - 1))
        )
        held = jnp.where(to_side, jnp.where(dx == 1, 0, 2) + place % 2, place)
        list_ref[spot] = held * per_device + slot % per_device
        one = lambda flag: jnp.where(flag, 1, 0)
        return near + one(to_near), side + one(to_side), rest + one(to_rest)

    zero = jnp.int32(0)
    near, side, rest = lax.fori_loop(0, kept_ref.shape[1], note, (zero, zero, zero), unroll=4)
    list_ref[3 * LIST] = near
    list_ref[3 * LIST + 1] = side
    list_ref[3 * LIST + 2] = rest


def page_lists(kept, slots, place, x_count):
    smem = pl.BlockSpec(memory_space=pltpu.SMEM)
    return pl.pallas_call(
        functools.partial(list_kernel, x_count),
        out_shape=jax.ShapeDtypeStruct((4 * LIST,), jnp.int32),
        in_specs=[smem] * 3,
        out_specs=smem,
    )(kept, slots, place)


def some_pages(list_ref, group, first, many, limit, k_ref, v_ref):
    ks, vs = [], []
    for j in range(many):
        page = list_ref[group * LIST + first + j]
        ks.append(k_ref[page])
        vs.append(v_ref[page])
    lane = lax.broadcasted_iota(jnp.int32, (1, many * PAGE), 1) // PAGE
    row = jnp.where(lane + first < limit, 0.0, MASKED)
    return jnp.concatenate(ks, axis=0), jnp.concatenate(vs, axis=0), row


def score(q_ref, g, keys, bias, rows=slice(None)):
    q = q_ref[rows, g * W : (g + 1) * W]
    return lax.dot_general(q, keys, (((1,), (1,)), ((), ())), preferred_element_type=F32) + bias()


def wide(tile, keys):
    return jnp.concatenate([tile] * (keys.shape[0] // W), axis=1)


def weigh(s, m, values):
    p = jnp.exp(s - m)
    sums = sum(p[:, c * W : (c + 1) * W] for c in range(p.shape[1] // W))
    return sums, jnp.dot(p.astype(BF16), values, preferred_element_type=F32)


def absorb(q_ref, g, keys, values, bias, acc_ref, m_ref, l_ref):
    s = score(q_ref, g, keys, bias)
    m_old = m_ref[g]
    m_new = jnp.maximum(m_old, jnp.max(s, axis=1, keepdims=True))
    rescale = jnp.exp(m_old - m_new)
    sums, summed = weigh(s, wide(m_new, keys), values)
    l_ref[g] = l_ref[g] * rescale + sums
    acc_ref[g] = acc_ref[g] * rescale + summed
    m_ref[g] = m_new


def gather_kernel(
    x_count,
    z_count,
    scale_base,
    list_ref,
    positions_ref,
    hidden_ref,
    w_query_ref,
    w_key_ref,
    w_value_ref,
    w_out_ref,
    keys_ref,
    values_ref,
    all_keys,
    all_values,
    queries,
    w_slab,
    acc_ref,
    m_ref,
    l_ref,
    hidden_vmem,
    wq_vmem,
    wk_vmem,
    wv_vmem,
    acc_vmem,
    q_vmem,
    new_vmem,
    all_new,
    near_k,
    near_v,
    side_k,
    side_v,
    bias_ref,
    stats_out,
    stats_in,
    send_sem,
    recv_sem,
    load_sem,
    local_sem,
):
    ctx, head, core, at = places(x_count)
    z, y_lo = head // 2, head % 2
    tokens = hidden_ref.shape[0]
    half = w_out_ref.shape[0] // 2
    columns = w_slab.shape[2]
    depth = hidden_ref.shape[1]
    steps = load_sem.shape[0]
    cut = depth // steps

    right, left, far = at(dx=1), at(dx=x_count - 1), at(dx=2)
    sibling, y_peer = at(dc=1), at(dy=1)
    cross = (ctx // 4 * 2 + lax.rem((ctx // 2) % 2 + core, 2)) * 2 + core
    out_peers = []
    for dz in range(z_count):
        for dl in range(2):
            if dz or dl:
                other = lax.rem(z + dz, z_count) * 2 + lax.rem(y_lo + dl, 2)
                back = lax.rem(z + z_count - dz, z_count) * 2 + lax.rem(y_lo + dl, 2)
                out_peers.append((cross if dl else ctx, other, back))

    barrier = pltpu.get_barrier_semaphore()
    met = [(c, head) for c in (right, left, far, sibling, y_peer)]
    met += [(c, h) for c, h, _ in out_peers]
    for device in met:
        pl.semaphore_signal(barrier, inc=1, device_id=device, device_id_type=MESH)
    pl.semaphore_wait(barrier, len(met))

    counter = [0]

    def send(source, target, device):
        i = counter[0]
        counter[0] += 1
        copy = pltpu.make_async_remote_copy(
            src_ref=source,
            dst_ref=target,
            send_sem=send_sem.at[i],
            recv_sem=recv_sem.at[i],
            device_id=device,
            device_id_type=MESH,
        )
        copy.start()
        return copy

    last = 2 * (x_count - 1)
    both = ((keys_ref, all_keys), (values_ref, all_values))
    thirds = [pl.ds(i * (keys_ref.shape[0] // PIECES), keys_ref.shape[0] // PIECES) for i in range(PIECES)]
    near = {}

    def send_near(i):
        for which, (mine, everyone) in enumerate(both):
            for slot, device in ((last, right), (2, left)):
                near[which, slot, i] = send(
                    mine.at[thirds[i]], everyone.at[slot, thirds[i]], (device, head)
                )

    send_near(0)
    my_half = pl.ds(pl.multiple_of(core * half, half), half)
    slabs = []
    for c, h, back in out_peers:
        cols = pl.ds(pl.multiple_of(h * columns, columns), columns)
        copy = send(w_out_ref.at[my_half, cols], w_slab.at[head, my_half], (c, h))
        slabs.append((copy, back))
    pair = [send(mine, everyone.at[1], (sibling, head)) for mine, everyone in both]
    loads = []
    for i in range(steps):
        rows = pl.ds(i * cut, cut)
        pieces = [
            pltpu.make_async_copy(hidden_ref.at[:, rows], hidden_vmem.at[:, rows], load_sem.at[i, 0]),
            pltpu.make_async_copy(w_query_ref.at[rows], wq_vmem.at[rows], load_sem.at[i, 1]),
            pltpu.make_async_copy(w_key_ref.at[rows], wk_vmem.at[rows], load_sem.at[i, 2]),
            pltpu.make_async_copy(w_value_ref.at[rows], wv_vmem.at[rows], load_sem.at[i, 3]),
        ]
        for piece in pieces:
            piece.start()
        loads.append(pieces)
    keep = keys_ref.shape[0]
    near_loads = [
        pltpu.make_async_copy(keys_ref, near_k.at[pl.ds(0, keep)], local_sem.at[5]),
        pltpu.make_async_copy(values_ref, near_v.at[pl.ds(0, keep)], local_sem.at[6]),
    ]
    for copy in near_loads:
        copy.start()

    q_cols = wq_vmem.shape[1]
    def project(pieces, parts):
        for i in range(steps):
            for piece in pieces:
                loads[i][piece].wait()
            rows = slice(i * cut, (i + 1) * cut)
            part = hidden_vmem[:, rows]
            for w_ref, first, end in parts:
                product = jnp.dot(part, w_ref[rows, :], preferred_element_type=F32)
                if i:
                    acc_vmem[:, first:end] += product
                else:
                    acc_vmem[:, first:end] = product

    project((0, 1), ((wq_vmem, 0, q_cols),))
    my_positions = positions_ref[pl.ds(ctx, 1), :]
    spread = jnp.broadcast_to(my_positions, (tokens, tokens))
    diagonal = lax.broadcasted_iota(jnp.int32, (tokens, tokens), 0) == lax.broadcasted_iota(
        jnp.int32, (tokens, tokens), 1
    )
    column = jnp.sum(jnp.where(diagonal, spread, 0).astype(F32), axis=1, keepdims=True)
    thousands = jnp.floor((column + (scale_base + 1.0)) * (1.0 / 8192.0))
    scaling = (jnp.log(thousands + 1.0) * 0.1 + 1.0) / math.sqrt(W)
    q_vmem[:tokens, :] = (acc_vmem[:, :q_cols] * scaling).astype(BF16)
    rows_own, rows_peer = pl.ds(0, tokens), pl.ds(tokens, tokens)
    ask = send(q_vmem.at[rows_own], q_vmem.at[rows_peer], (y_peer, head))
    project((2, 3), ((wk_vmem, q_cols, q_cols + W), (wv_vmem, q_cols + W, q_cols + 2 * W)))
    new_vmem[...] = acc_vmem[:, q_cols:].astype(BF16)
    fresh = [
        send(new_vmem, all_new.at[last], (right, head)),
        send(new_vmem, all_new.at[2], (left, head)),
        send(new_vmem, all_new.at[4], (far, head)),
    ]
    fresh_pair = [send(new_vmem, all_new.at[1], (sibling, head))]
    all_new[0] = new_vmem[...]
    for i in range(1, PIECES):
        send_near(i)

    def positions_of(which):
        return positions_ref[pl.ds(which, 1), :].astype(F32)

    def as_column(row):
        spread = jnp.where(diagonal, jnp.broadcast_to(row, (tokens, tokens)), 0.0)
        return jnp.sum(spread, axis=1, keepdims=True)

    mine = jnp.concatenate([column, as_column(positions_of(y_peer))], axis=0)
    for slot in range(2 * x_count):
        theirs = positions_of(at(dx=slot // 2, dc=slot % 2))
        bias_ref[slot // 4, :, (slot % 4) * tokens : (slot % 4 + 1) * tokens] = jnp.where(
            theirs > mine, MASKED, 0.0
        )

    for copy, everyone, held, sem in zip(pair[:2], (all_keys, all_values), (near_k, near_v), (7, 8)):
        copy.wait_recv()
        load = pltpu.make_async_copy(everyone.at[1], held.at[pl.ds(keep, keep)], local_sem.at[sem])
        load.start()
        near_loads.append(load)
    for load in near_loads:
        load.wait()
    own = [
        pltpu.make_async_copy(held.at[pl.ds(0, keep)], everyone.at[0], local_sem.at[i])
        for i, (held, everyone) in enumerate(((near_k, all_keys), (near_v, all_values)))
    ]
    for copy in own:
        copy.start()

    near_args = (list_ref, 0, 0, NEAR, list_ref[3 * LIST], near_k, near_v)

    def new_block(b):
        pieces = [all_new[4 * b + j] for j in range(4)]
        block = jnp.concatenate(pieces, axis=0)
        return block[:, :W], block[:, W:], lambda: bias_ref[b]

    def peaks_of(rows):
        here = slice(rows * tokens, (rows + 1) * tokens)
        keys, _, row = some_pages(*near_args)
        for g in range(G):
            s = score(q_vmem, g, keys, lambda: row, here)
            m_ref[g, here] = jnp.maximum(
                jnp.max(s, axis=1, keepdims=True), jnp.full((tokens, W), LOW, F32)
            )
        if rows == 0:
            for copy, slot in zip(fresh, (last, 2, 4)):
                copy.wait_recv()
                fresh_pair.append(send(all_new.at[slot], all_new.at[slot + 1], (sibling, head)))
            for copy in fresh_pair:
                copy.wait_recv()

        def new_peak(b, _):
            keys, _, _ = new_block(b)
            for g in range(G):
                s = score(q_vmem, g, keys, lambda: bias_ref[b, here], here)
                m_ref[g, here] = jnp.maximum(m_ref[g, here], jnp.max(s, axis=1, keepdims=True))
            return 0

        lax.fori_loop(0, x_count // 2, new_peak, 0)

    peaks_of(0)
    ask.wait_recv()
    late = [pltpu.make_async_copy(q_vmem, queries, local_sem.at[3])]
    late[0].start()
    peaks_of(1)
    lane = lax.broadcasted_iota(jnp.int32, (2 * tokens, W), 1)
    stats = jnp.zeros((2 * tokens, W), F32)
    for g in range(G):
        stats = jnp.where(lane == g, m_ref[g], stats)
    stats_out[...] = stats.T[:8]
    peaks = send(stats_out, stats_in, (y_peer, head))

    across, near_pair, side_loads = [], [], []

    def pass_on(i):
        for which, (_, everyone) in enumerate(both):
            for slot in (last, 2):
                near[which, slot, i].wait_recv()
                here = everyone.at[slot, thirds[i]]
                if which == 0 and slot == last:
                    across.append(send(here, everyone.at[4, thirds[i]], (right, head)))
                if which == 1 and slot == 2:
                    across.append(send(here, everyone.at[4, thirds[i]], (left, head)))
                near_pair.append(send(here, everyone.at[slot + 1, thirds[i]], (sibling, head)))

    pass_on(0)
    peaks.wait_recv()
    their_peaks = jnp.concatenate([stats_in[...]] * (W // 8), axis=0).T
    for g in range(G):
        theirs = their_peaks[:, g : g + 1]
        theirs = jnp.concatenate([theirs[tokens:], theirs[:tokens]], axis=0)
        m_ref[g] = jnp.maximum(m_ref[g], theirs)

    keys, values, row = some_pages(*near_args)
    for g in range(G):
        l_ref[g], acc_ref[g] = weigh(score(q_vmem, g, keys, lambda: row), wide(m_ref[g], keys), values)

    for i in range(1, PIECES):
        pass_on(i)

    def hold(odd):
        for which, (_, everyone) in enumerate(both):
            for spot, slot in ((0, 2), (2, last)):
                load = pltpu.make_async_copy(
                    everyone.at[slot + odd],
                    (side_k, side_v)[which].at[pl.ds((spot + odd) * keep, keep)],
                    local_sem.at[9 + len(side_loads)],
                )
                load.start()
                side_loads.append(load)

    hold(0)

    def new_weights(b, _):
        keys, values, bias = new_block(b)
        for g in range(G):
            sums, summed = weigh(score(q_vmem, g, keys, bias), wide(m_ref[g], keys), values)
            l_ref[g] += sums
            acc_ref[g] += summed
        return 0

    lax.fori_loop(0, x_count // 2, new_weights, 0)

    for copy in near_pair:
        copy.wait_recv()
    hold(1)
    for load in side_loads:
        load.wait()
    keys, values, row = some_pages(list_ref, 1, 0, SIDE, list_ref[3 * LIST + 1], side_k, side_v)
    for g in range(G):
        absorb(q_vmem, g, keys, values, lambda: row, acc_ref, m_ref, l_ref)

    across_pair = []
    for i, copy in enumerate(across):
        copy.wait_recv()
        everyone, here = both[i % 2][1], thirds[i // 2]
        across_pair.append(send(everyone.at[4, here], everyone.at[5, here], (sibling, head)))
    slab_pair = []
    for copy, back in slabs:
        copy.wait_recv()
        slab_pair.append(send(w_slab.at[back, my_half], w_slab.at[back, my_half], (sibling, head)))
    for copy in across_pair + slab_pair:
        copy.wait_recv()
    for copy in list(near.values()) + pair + fresh + fresh_pair + across + near_pair + across_pair:
        copy.wait_send()
    for copy in slab_pair + [ask, peaks]:
        copy.wait_send()
    for copy, _ in slabs:
        copy.wait_send()
    for copy in own + late:
        copy.wait()


def gather(lists, positions, hidden, w_query, w_key, w_value, w_out, keys, values, x_count, z_count):
    held = keys.shape[0]
    tokens, depth = hidden.shape
    q_cols = w_query.shape[1]
    columns = w_out.shape[1] // (2 * z_count)
    anywhere = pl.BlockSpec(memory_space=pl.ANY)
    vmem = pl.BlockSpec(memory_space=pltpu.VMEM)
    steps = 5
    copies = 64
    state = jax.ShapeDtypeStruct((G, 2 * tokens, W), F32)
    return pl.pallas_call(
        functools.partial(gather_kernel, x_count, z_count, float(held * PAGE * x_count * 4)),
        out_shape=[
            jax.ShapeDtypeStruct((2 * x_count, held, PAGE, W), BF16),
            jax.ShapeDtypeStruct((2 * x_count, held, PAGE, W), BF16),
            jax.ShapeDtypeStruct((2 * tokens, q_cols), BF16),
            jax.ShapeDtypeStruct((2 * z_count, w_out.shape[0], columns), BF16),
            state,
            state,
            state,
        ],
        in_specs=[pl.BlockSpec(memory_space=pltpu.SMEM), vmem] + [anywhere] * 7,
        out_specs=[anywhere] * 4 + [vmem] * 3,
        scratch_shapes=[
            pltpu.VMEM((tokens, depth), BF16),
            pltpu.VMEM((depth, q_cols), BF16),
            pltpu.VMEM((depth, W), BF16),
            pltpu.VMEM((depth, W), BF16),
            pltpu.VMEM((tokens, q_cols + 2 * W), F32),
            pltpu.VMEM((2 * tokens, q_cols), BF16),
            pltpu.VMEM((tokens, 2 * W), BF16),
            pltpu.VMEM((2 * x_count, tokens, 2 * W), BF16),
            pltpu.VMEM((2 * held, PAGE, W), BF16),
            pltpu.VMEM((2 * held, PAGE, W), BF16),
            pltpu.VMEM((4 * held, PAGE, W), BF16),
            pltpu.VMEM((4 * held, PAGE, W), BF16),
            pltpu.VMEM((x_count // 2, 2 * tokens, 4 * tokens), F32),
            pltpu.VMEM((8, 2 * tokens), F32),
            pltpu.VMEM((8, 2 * tokens), F32),
            pltpu.SemaphoreType.DMA((copies,)),
            pltpu.SemaphoreType.DMA((copies,)),
            pltpu.SemaphoreType.DMA((steps, 4)),
            pltpu.SemaphoreType.DMA((17,)),
        ],
        compiler_params=pltpu.CompilerParams(
            collective_id=0, has_side_effects=True, vmem_limit_bytes=60 * 2**20
        ),
    )(lists, positions, hidden, w_query, w_key, w_value, w_out, keys, values)


def extra_kernel(
    list_ref, q_any, k_any, v_any, acc_in, m_in, l_in, acc_any, m_any, l_any, q, k, v, acc, m, l, sem
):
    count = list_ref[3 * LIST + 2]

    @pl.when(count > REST)
    def _():
        pairs = [(q_any, q), (k_any, k), (v_any, v), (acc_any, acc), (m_any, m), (l_any, l)]
        copies = [pltpu.make_async_copy(a, b, sem.at[i]) for i, (a, b) in enumerate(pairs)]
        for copy in copies:
            copy.start()
        for copy in copies:
            copy.wait()

        def step(i, _):
            keys, values, row = some_pages(list_ref, 2, REST + i * 4, 4, count, k, v)
            for g in range(G):
                absorb(q, g, keys, values, lambda: row, acc, m, l)
            return 0

        lax.fori_loop(0, (count - REST + 3) // 4, step, 0)
        back = [pltpu.make_async_copy(b, a, sem.at[i]) for i, (a, b) in enumerate(pairs[3:])]
        for copy in back:
            copy.start()
        for copy in back:
            copy.wait()


def extra(lists, queries, keys, values, acc, m, l):
    anywhere = pl.BlockSpec(memory_space=pl.ANY)
    state = jax.ShapeDtypeStruct(acc.shape, F32)
    return pl.pallas_call(
        extra_kernel,
        out_shape=[state] * 3,
        in_specs=[pl.BlockSpec(memory_space=pltpu.SMEM)] + [anywhere] * 6,
        out_specs=[anywhere] * 3,
        input_output_aliases={4: 0, 5: 1, 6: 2},
        scratch_shapes=[
            pltpu.VMEM(queries.shape, BF16),
            pltpu.VMEM(keys.shape, BF16),
            pltpu.VMEM(values.shape, BF16),
            pltpu.VMEM(acc.shape, F32),
            pltpu.VMEM(acc.shape, F32),
            pltpu.VMEM(acc.shape, F32),
            pltpu.SemaphoreType.DMA((6,)),
        ],
        compiler_params=pltpu.CompilerParams(vmem_limit_bytes=60 * 2**20),
    )(lists, queries, keys, values, acc, m, l)


def finish_kernel(
    x_count,
    z_count,
    list_ref,
    q_any,
    k_any,
    v_any,
    acc_any,
    m_any,
    l_any,
    w_out_ref,
    slab_ref,
    out_ref,
    q_ref,
    k_ref,
    v_ref,
    acc_ref,
    m_ref,
    l_ref,
    acc_in,
    stats_out,
    stats_in,
    slab_vmem,
    heads,
    send_sem,
    recv_sem,
    load_sem,
):
    ctx, head, core, at = places(x_count)
    z, y_lo = head // 2, head % 2
    tokens = acc_in.shape[1]
    y_peer = at(dy=1)

    def head_at(dz, dl):
        return lax.rem(z + dz, z_count) * 2 + lax.rem(y_lo + dl, 2)

    above, below, beside = head_at(1, 0), head_at(z_count - 1, 0), head_at(0, 1)
    loads = [
        pltpu.make_async_copy(source, target, load_sem.at[i])
        for i, (source, target) in enumerate(
            [
                (q_any, q_ref),
                (k_any, k_ref),
                (v_any, v_ref),
                (acc_any, acc_ref),
                (m_any, m_ref),
                (l_any, l_ref),
            ]
        )
    ]
    columns = slab_ref.shape[2]
    my_cols = pl.ds(pl.multiple_of(head * columns, columns), columns)
    weights = [pltpu.make_async_copy(w_out_ref.at[:, my_cols], slab_vmem.at[head], load_sem.at[6])]
    for i in range(1, 2 * z_count):
        which = lax.rem(head + i, 2 * z_count)
        weights.append(
            pltpu.make_async_copy(slab_ref.at[which], slab_vmem.at[which], load_sem.at[6 + i])
        )
    for load in loads + weights:
        load.start()

    barrier = pltpu.get_barrier_semaphore()
    met = [(y_peer, head), (ctx, above), (ctx, below), (ctx, beside)]
    for device in met:
        pl.semaphore_signal(barrier, inc=1, device_id=device, device_id_type=MESH)
    pl.semaphore_wait(barrier, len(met))

    counter = [0]
    started = []

    def send(source, target, device):
        i = counter[0]
        counter[0] += 1
        copy = pltpu.make_async_remote_copy(
            src_ref=source,
            dst_ref=target,
            send_sem=send_sem.at[i],
            recv_sem=recv_sem.at[i],
            device_id=device,
            device_id_type=MESH,
        )
        copy.start()
        started.append(copy)
        return copy

    rows_peer = pl.ds(tokens, tokens)
    lane_row = lax.broadcasted_iota(jnp.int32, (tokens, W), 1)
    for load in loads:
        load.wait()
    blocks = [
        some_pages(list_ref, 2, first, BLOCK, list_ref[3 * LIST + 2], k_ref, v_ref)
        for first in range(0, REST, BLOCK)
    ]
    stats_copies, parts = [], []

    def attend(g):
        for keys, values, row in blocks:
            absorb(q_ref, g, keys, values, lambda: row, acc_ref, m_ref, l_ref)
        l_ref[g] = jnp.broadcast_to(jnp.sum(l_ref[g], axis=1, keepdims=True), l_ref.shape[1:])
        stats_out[g] = jnp.where(lane_row == 0, m_ref[g, tokens:], l_ref[g, tokens:]).T[:8]
        stats_copies.append(send(stats_out.at[g], stats_in.at[g], (y_peer, head)))
        parts.append(send(acc_ref.at[g, rows_peer], acc_in.at[g], (y_peer, head)))

    def pass_on(who, g, device):
        return send(heads.at[who, g], heads.at[who, g], (ctx, device))

    first = [True]

    def use_first(who, g):
        if first[0]:
            for load in weights:
                load.wait()
        use_now(who, g)

    def use_now(who, g):
        product = jnp.dot(
            heads[who, g], slab_vmem[who, g * W : (g + 1) * W, :], preferred_element_type=F32
        )
        if first[0]:
            out_ref[...] = product
            first[0] = False
        else:
            out_ref[...] += product

    up, down, side, up_side, down_side, two, two_side = ({} for _ in range(7))
    attend(0)
    for t in range(G + 3):
        g = t
        if g + 1 < G:
            attend(g + 1)
        if g < G:
            stats_copies[g].wait_recv()
            parts[g].wait_recv()
            m1, l1 = m_ref[g, :tokens], l_ref[g, :tokens]
            theirs = jnp.concatenate([stats_in[g]] * (W // 8), axis=0).T
            m2, l2 = theirs[:, 0:1], theirs[:, 1:2]
            m = jnp.maximum(m1, m2)
            a1, a2 = jnp.exp(m1 - m), jnp.exp(m2 - m)
            total = l1 * a1 + l2 * a2
            heads[head, g] = (acc_ref[g, :tokens] * (a1 / total) + acc_in[g] * (a2 / total)).astype(BF16)
            side[g] = pass_on(head, g, beside)
            up[g] = pass_on(head, g, above)
            down[g] = pass_on(head, g, below)
            use_first(head, g)
        g = t - 1
        if 0 <= g < G:
            side[g].wait_recv()
            up_side[g] = pass_on(beside, g, above)
            down_side[g] = pass_on(beside, g, below)
            up[g].wait_recv()
            down[g].wait_recv()
            if g % 2 == 0:
                two[g] = pass_on(below, g, above)
            else:
                two[g] = pass_on(above, g, below)
            use_now(beside, g)
            use_now(below, g)
            use_now(above, g)
        g = t - 2
        if 0 <= g < G:
            up_side[g].wait_recv()
            down_side[g].wait_recv()
            if g % 2 == 1:
                two_side[g] = pass_on(head_at(z_count - 1, 1), g, above)
            else:
                two_side[g] = pass_on(head_at(1, 1), g, below)
            use_now(head_at(z_count - 1, 1), g)
            use_now(head_at(1, 1), g)
        g = t - 3
        if 0 <= g < G:
            two[g].wait_recv()
            use_now(head_at(2, 0), g)
            two_side[g].wait_recv()
            use_now(head_at(2, 1), g)
    for copy in started:
        copy.wait_send()


def finish(lists, queries, keys, values, acc, m, l, w_out, slab, x_count, z_count):
    tokens = queries.shape[0] // 2
    anywhere = pl.BlockSpec(memory_space=pl.ANY)
    copies = G * 9
    return pl.pallas_call(
        functools.partial(finish_kernel, x_count, z_count),
        out_shape=jax.ShapeDtypeStruct((tokens, slab.shape[2]), F32),
        in_specs=[pl.BlockSpec(memory_space=pltpu.SMEM)] + [anywhere] * 8,
        out_specs=pl.BlockSpec(memory_space=pltpu.VMEM),
        scratch_shapes=[
            pltpu.VMEM(queries.shape, BF16),
            pltpu.VMEM(keys.shape, BF16),
            pltpu.VMEM(values.shape, BF16),
            pltpu.VMEM(acc.shape, F32),
            pltpu.VMEM(acc.shape, F32),
            pltpu.VMEM(acc.shape, F32),
            pltpu.VMEM((G, tokens, W), F32),
            pltpu.VMEM((G, 8, tokens), F32),
            pltpu.VMEM((G, 8, tokens), F32),
            pltpu.VMEM(slab.shape, BF16),
            pltpu.VMEM((2 * z_count, G, tokens, W), BF16),
            pltpu.SemaphoreType.DMA((copies,)),
            pltpu.SemaphoreType.DMA((copies,)),
            pltpu.SemaphoreType.DMA((6 + 2 * z_count,)),
        ],
        compiler_params=pltpu.CompilerParams(
            collective_id=1, has_side_effects=True, vmem_limit_bytes=60 * 2**20
        ),
    )(lists, queries, keys, values, acc, m, l, w_out, slab)


def on_device(
    hidden,
    positions,
    w_query,
    key_matrix,
    value_matrix,
    w_out,
    stored_keys,
    stored_values,
    kept_pages,
    page_slot,
):
    tokens = hidden.shape[0]
    ctx_count, head_count = lax.axis_size("ctx"), lax.axis_size("head")
    x_count, z_count = ctx_count // 4, head_count // 2
    ctx, head = lax.axis_index("ctx"), lax.axis_index("head")
    table = positions.reshape(ctx_count, tokens)
    place = jnp.stack([ctx, head]).astype(jnp.int32)
    lists = page_lists(kept_pages, page_slot, place, x_count)
    keys, values, queries, slab, acc, m, l = gather(
        lists, table, hidden, w_query, key_matrix, value_matrix, w_out,
        stored_keys.reshape(-1, PAGE, W), stored_values.reshape(-1, PAGE, W),
        x_count, z_count,
    )
    keys, values = keys.reshape(-1, PAGE, W), values.reshape(-1, PAGE, W)
    acc, m, l = extra(lists, queries, keys, values, acc, m, l)
    return finish(lists, queries, keys, values, acc, m, l, w_out, slab, x_count, z_count)


def solution(mesh):
    placed = (
        P("ctx", None),
        P(),
        P(None, "head"),
        P(None, "head"),
        P(None, "head"),
        P("head", None),
        P("ctx", "head"),
        P("ctx", "head"),
        P(),
        P(),
    )
    return jax.shard_map(
        on_device, mesh=mesh, in_specs=placed, out_specs=P("ctx", "head"), check_vma=False
    )
```

```python
import functools
import math

import jax
import jax.numpy as jnp
from jax import lax
from jax.experimental import pallas as pl
from jax.experimental.pallas import tpu as pltpu
from jax.sharding import PartitionSpec as P

G = 5
W = 128
PAGE = 128
LOW = -1e30
MASKED = -3e38
BLOCK = 12
NEAR = 12
SIDE = 12
REST = 36
LIST = 128
PIECES = 3
MESH = pl.DeviceIdType.MESH
F32 = jnp.float32
BF16 = jnp.bfloat16


def places(x_count):
    ctx = lax.axis_index("ctx")
    head = lax.axis_index("head")
    x, y_hi, core = ctx // 4, (ctx // 2) % 2, ctx % 2

    def at(dx=0, dy=0, dc=0):
        return (lax.rem(x + dx, x_count) * 2 + lax.rem(y_hi + dy, 2)) * 2 + lax.rem(core + dc, 2)

    return ctx, head, core, at


def list_kernel(x_count, kept_ref, slot_ref, list_ref):
    ctx, head = lax.axis_index("ctx"), lax.axis_index("head")
    x, y_hi, core = ctx // 4, (ctx // 2) % 2, ctx % 2
    slots = slot_ref.shape[0]
    per_device = slots // (4 * x_count)
    inverse = -(-65536 // per_device)
    assert all(i * inverse >> 16 == i // per_device for i in range(slots))
    assert x_count & (x_count - 1) == 0

    for first, many in ((0, NEAR), (LIST, SIDE), (2 * LIST, kept_ref.shape[1] + 4)):
        for i in range(many):
            list_ref[first + i] = 0

    def note(i, counts):
        near, side, rest = counts
        slot = slot_ref[kept_ref[head, i]]
        where = (slot * inverse) >> 16
        dx = ((where >> 2) - x) & (x_count - 1)
        dc = (where ^ core) & 1
        ours = ((where >> 1) & 1) == y_hi
        to_near = ours & (dx == 0) & (near < NEAR)
        to_side = ours & ((dx & 1) == 1) & (side < SIDE)
        to_rest = ours & jnp.logical_not(to_near | to_side)
        spot = jnp.where(
            to_near, near, jnp.where(to_side, LIST + side, jnp.where(to_rest, 2 * LIST + rest, 4 * LIST - 1))
        )
        held = jnp.where(to_side, dx - 1, 2 * dx) + dc
        list_ref[spot] = held * per_device + slot - where * per_device
        return near + to_near.astype(jnp.int32), side + to_side.astype(jnp.int32), rest + to_rest.astype(jnp.int32)

    zero = jnp.int32(0)
    near, side, rest = lax.fori_loop(0, kept_ref.shape[1], note, (zero, zero, zero), unroll=8)
    list_ref[3 * LIST] = near
    list_ref[3 * LIST + 1] = side
    list_ref[3 * LIST + 2] = rest


def page_lists(kept, slots, x_count):
    smem = pl.BlockSpec(memory_space=pltpu.SMEM)
    return pl.pallas_call(
        functools.partial(list_kernel, x_count),
        out_shape=jax.ShapeDtypeStruct((4 * LIST,), jnp.int32),
        in_specs=[smem] * 2,
        out_specs=smem,
    )(kept, slots)


def some_pages(list_ref, group, first, many, limit, k_ref, v_ref):
    ks, vs = [], []
    for j in range(many):
        page = list_ref[group * LIST + first + j]
        ks.append(k_ref[page])
        vs.append(v_ref[page])
    lane = lax.broadcasted_iota(jnp.int32, (1, many * PAGE), 1) // PAGE
    row = jnp.where(lane + first < limit, 0.0, MASKED)
    return jnp.concatenate(ks, axis=0), jnp.concatenate(vs, axis=0), row


def score(q_ref, g, keys, bias, rows=slice(None)):
    q = q_ref[rows, g * W : (g + 1) * W]
    return lax.dot_general(q, keys, (((1,), (1,)), ((), ())), preferred_element_type=F32) + bias()


def wide(tile, keys):
    return jnp.concatenate([tile] * (keys.shape[0] // W), axis=1)


def weigh(s, m, values):
    p = jnp.exp(s - m)
    sums = sum(p[:, c * W : (c + 1) * W] for c in range(p.shape[1] // W))
    return sums, jnp.dot(p.astype(BF16), values, preferred_element_type=F32)


def absorb(q_ref, g, keys, values, bias, acc_ref, m_ref, l_ref):
    s = score(q_ref, g, keys, bias)
    m_old = m_ref[g]
    m_new = jnp.maximum(m_old, jnp.max(s, axis=1, keepdims=True))
    rescale = jnp.exp(m_old - m_new)
    sums, summed = weigh(s, wide(m_new, keys), values)
    l_ref[g] = l_ref[g] * rescale + sums
    acc_ref[g] = acc_ref[g] * rescale + summed
    m_ref[g] = m_new


def gather_kernel(
    x_count,
    z_count,
    scale_base,
    list_ref,
    positions_ref,
    hidden_ref,
    w_query_ref,
    w_key_ref,
    w_value_ref,
    w_out_ref,
    keys_ref,
    values_ref,
    all_keys,
    all_values,
    queries,
    w_slab,
    acc_ref,
    m_ref,
    l_ref,
    hidden_vmem,
    wq_vmem,
    wk_vmem,
    wv_vmem,
    acc_vmem,
    q_vmem,
    new_vmem,
    all_new,
    near_k,
    near_v,
    side_k,
    side_v,
    bias_ref,
    stats_out,
    stats_in,
    send_sem,
    recv_sem,
    load_sem,
    local_sem,
):
    ctx, head, core, at = places(x_count)
    z, y_lo = head // 2, head % 2
    tokens = hidden_ref.shape[0]
    half = w_out_ref.shape[0] // 2
    columns = w_slab.shape[2]
    depth = hidden_ref.shape[1]
    steps = load_sem.shape[0]
    cut = depth // steps

    right, left, far = at(dx=1), at(dx=x_count - 1), at(dx=2)
    sibling, y_peer = at(dc=1), at(dy=1)
    cross = (ctx // 4 * 2 + lax.rem((ctx // 2) % 2 + core, 2)) * 2 + core
    out_peers = []
    for dz in range(z_count):
        for dl in range(2):
            if dz or dl:
                other = lax.rem(z + dz, z_count) * 2 + lax.rem(y_lo + dl, 2)
                back = lax.rem(z + z_count - dz, z_count) * 2 + lax.rem(y_lo + dl, 2)
                out_peers.append((cross if dl else ctx, other, back))

    barrier = pltpu.get_barrier_semaphore()
    met = [(c, head) for c in (right, left, far, sibling, y_peer)]
    met += [(c, h) for c, h, _ in out_peers]
    for device in met:
        pl.semaphore_signal(barrier, inc=1, device_id=device, device_id_type=MESH)
    pl.semaphore_wait(barrier, len(met))

    counter = [0]

    def send(source, target, device):
        i = counter[0]
        counter[0] += 1
        copy = pltpu.make_async_remote_copy(
            src_ref=source,
            dst_ref=target,
            send_sem=send_sem.at[i],
            recv_sem=recv_sem.at[i],
            device_id=device,
            device_id_type=MESH,
        )
        copy.start()
        return copy

    last = 2 * (x_count - 1)
    both = ((keys_ref, all_keys), (values_ref, all_values))
    thirds = [pl.ds(i * (keys_ref.shape[0] // PIECES), keys_ref.shape[0] // PIECES) for i in range(PIECES)]
    near = {}

    def send_near(i):
        for which, (mine, everyone) in enumerate(both):
            for slot, device in ((last, right), (2, left)):
                near[which, slot, i] = send(
                    mine.at[thirds[i]], everyone.at[slot, thirds[i]], (device, head)
                )

    send_near(0)
    my_half = pl.ds(pl.multiple_of(core * half, half), half)
    slabs = []
    for c, h, back in out_peers:
        cols = pl.ds(pl.multiple_of(h * columns, columns), columns)
        copy = send(w_out_ref.at[my_half, cols], w_slab.at[head, my_half], (c, h))
        slabs.append((copy, back))
    pair = [send(mine, everyone.at[1], (sibling, head)) for mine, everyone in both]
    loads = []
    for i in range(steps):
        rows = pl.ds(i * cut, cut)
        pieces = [
            pltpu.make_async_copy(hidden_ref.at[:, rows], hidden_vmem.at[:, rows], load_sem.at[i, 0]),
            pltpu.make_async_copy(w_query_ref.at[rows], wq_vmem.at[rows], load_sem.at[i, 1]),
            pltpu.make_async_copy(w_key_ref.at[rows], wk_vmem.at[rows], load_sem.at[i, 2]),
            pltpu.make_async_copy(w_value_ref.at[rows], wv_vmem.at[rows], load_sem.at[i, 3]),
        ]
        for piece in pieces:
            piece.start()
        loads.append(pieces)
    keep = keys_ref.shape[0]
    near_loads = [
        pltpu.make_async_copy(keys_ref, near_k.at[pl.ds(0, keep)], local_sem.at[5]),
        pltpu.make_async_copy(values_ref, near_v.at[pl.ds(0, keep)], local_sem.at[6]),
    ]
    for copy in near_loads:
        copy.start()

    q_cols = wq_vmem.shape[1]
    def project(pieces, parts):
        for i in range(steps):
            for piece in pieces:
                loads[i][piece].wait()
            rows = slice(i * cut, (i + 1) * cut)
            part = hidden_vmem[:, rows]
            for w_ref, first, end in parts:
                product = jnp.dot(part, w_ref[rows, :], preferred_element_type=F32)
                if i:
                    acc_vmem[:, first:end] += product
                else:
                    acc_vmem[:, first:end] = product

    project((0, 1), ((wq_vmem, 0, q_cols),))

    def position_row(which):
        lines = [positions_ref[pl.ds(which * (tokens // W) + i, 1), :] for i in range(tokens // W)]
        return jnp.concatenate(lines, axis=1)

    my_positions = position_row(ctx)
    spread = jnp.broadcast_to(my_positions, (tokens, tokens))
    diagonal = lax.broadcasted_iota(jnp.int32, (tokens, tokens), 0) == lax.broadcasted_iota(
        jnp.int32, (tokens, tokens), 1
    )
    column = jnp.sum(jnp.where(diagonal, spread, 0).astype(F32), axis=1, keepdims=True)
    thousands = jnp.floor((column + (scale_base + 1.0)) * (1.0 / 8192.0))
    scaling = (jnp.log(thousands + 1.0) * 0.1 + 1.0) / math.sqrt(W)
    q_vmem[:tokens, :] = (acc_vmem[:, :q_cols] * scaling).astype(BF16)
    rows_own, rows_peer = pl.ds(0, tokens), pl.ds(tokens, tokens)
    ask = send(q_vmem.at[rows_own], q_vmem.at[rows_peer], (y_peer, head))
    project((2, 3), ((wk_vmem, q_cols, q_cols + W), (wv_vmem, q_cols + W, q_cols + 2 * W)))
    new_vmem[...] = acc_vmem[:, q_cols:].astype(BF16)
    fresh = [
        send(new_vmem, all_new.at[last], (right, head)),
        send(new_vmem, all_new.at[2], (left, head)),
        send(new_vmem, all_new.at[4], (far, head)),
    ]
    fresh_pair = [send(new_vmem, all_new.at[1], (sibling, head))]
    all_new[0] = new_vmem[...]
    for i in range(1, PIECES):
        send_near(i)

    def positions_of(which):
        return position_row(which).astype(F32)

    def as_column(row):
        spread = jnp.where(diagonal, jnp.broadcast_to(row, (tokens, tokens)), 0.0)
        return jnp.sum(spread, axis=1, keepdims=True)

    mine = jnp.concatenate([column, as_column(positions_of(y_peer))], axis=0)
    for slot in range(2 * x_count):
        theirs = positions_of(at(dx=slot // 2, dc=slot % 2))
        bias_ref[slot // 4, :, (slot % 4) * tokens : (slot % 4 + 1) * tokens] = jnp.where(
            theirs > mine, MASKED, 0.0
        )

    for copy, everyone, held, sem in zip(pair[:2], (all_keys, all_values), (near_k, near_v), (7, 8)):
        copy.wait_recv()
        load = pltpu.make_async_copy(everyone.at[1], held.at[pl.ds(keep, keep)], local_sem.at[sem])
        load.start()
        near_loads.append(load)
    for load in near_loads:
        load.wait()
    own = [
        pltpu.make_async_copy(held.at[pl.ds(0, keep)], everyone.at[0], local_sem.at[i])
        for i, (held, everyone) in enumerate(((near_k, all_keys), (near_v, all_values)))
    ]
    for copy in own:
        copy.start()

    near_args = (list_ref, 0, 0, NEAR, list_ref[3 * LIST], near_k, near_v)

    def new_block(b):
        pieces = [all_new[4 * b + j] for j in range(4)]
        block = jnp.concatenate(pieces, axis=0)
        return block[:, :W], block[:, W:], lambda: bias_ref[b]

    def peaks_of(rows):
        here = slice(rows * tokens, (rows + 1) * tokens)
        keys, _, row = some_pages(*near_args)
        for g in range(G):
            s = score(q_vmem, g, keys, lambda: row, here)
            m_ref[g, here] = jnp.maximum(
                jnp.max(s, axis=1, keepdims=True), jnp.full((tokens, W), LOW, F32)
            )
        if rows == 0:
            for copy, slot in zip(fresh, (last, 2, 4)):
                copy.wait_recv()
                fresh_pair.append(send(all_new.at[slot], all_new.at[slot + 1], (sibling, head)))
            for copy in fresh_pair:
                copy.wait_recv()

        def new_peak(b, _):
            keys, _, _ = new_block(b)
            for g in range(G):
                s = score(q_vmem, g, keys, lambda: bias_ref[b, here], here)
                m_ref[g, here] = jnp.maximum(m_ref[g, here], jnp.max(s, axis=1, keepdims=True))
            return 0

        lax.fori_loop(0, x_count // 2, new_peak, 0)

    peaks_of(0)
    ask.wait_recv()
    late = [pltpu.make_async_copy(q_vmem, queries, local_sem.at[3])]
    late[0].start()
    peaks_of(1)
    lane = lax.broadcasted_iota(jnp.int32, (2 * tokens, W), 1)
    stats = jnp.zeros((2 * tokens, W), F32)
    for g in range(G):
        stats = jnp.where(lane == g, m_ref[g], stats)
    stats_out[...] = stats.T[:8]
    peaks = send(stats_out, stats_in, (y_peer, head))

    across, near_pair, side_loads = [], [], []

    def pass_on(i):
        for which, (_, everyone) in enumerate(both):
            for slot in (last, 2):
                near[which, slot, i].wait_recv()
                here = everyone.at[slot, thirds[i]]
                if which == 0 and slot == last:
                    across.append(send(here, everyone.at[4, thirds[i]], (right, head)))
                if which == 1 and slot == 2:
                    across.append(send(here, everyone.at[4, thirds[i]], (left, head)))
                near_pair.append(send(here, everyone.at[slot + 1, thirds[i]], (sibling, head)))

    pass_on(0)
    peaks.wait_recv()
    their_peaks = jnp.concatenate([stats_in[...]] * (W // 8), axis=0).T
    for g in range(G):
        theirs = their_peaks[:, g : g + 1]
        theirs = jnp.concatenate([theirs[tokens:], theirs[:tokens]], axis=0)
        m_ref[g] = jnp.maximum(m_ref[g], theirs)

    keys, values, row = some_pages(*near_args)
    for g in range(G):
        l_ref[g], acc_ref[g] = weigh(score(q_vmem, g, keys, lambda: row), wide(m_ref[g], keys), values)

    for i in range(1, PIECES):
        pass_on(i)

    def hold(odd):
        for which, (_, everyone) in enumerate(both):
            for spot, slot in ((0, 2), (2, last)):
                load = pltpu.make_async_copy(
                    everyone.at[slot + odd],
                    (side_k, side_v)[which].at[pl.ds((spot + odd) * keep, keep)],
                    local_sem.at[9 + len(side_loads)],
                )
                load.start()
                side_loads.append(load)

    hold(0)

    def new_weights(b, _):
        keys, values, bias = new_block(b)
        for g in range(G):
            sums, summed = weigh(score(q_vmem, g, keys, bias), wide(m_ref[g], keys), values)
            l_ref[g] += sums
            acc_ref[g] += summed
        return 0

    lax.fori_loop(0, x_count // 2, new_weights, 0)

    for copy in near_pair:
        copy.wait_recv()
    hold(1)
    for load in side_loads:
        load.wait()
    keys, values, row = some_pages(list_ref, 1, 0, SIDE, list_ref[3 * LIST + 1], side_k, side_v)
    for g in range(G):
        absorb(q_vmem, g, keys, values, lambda: row, acc_ref, m_ref, l_ref)

    across_pair = []
    for i, copy in enumerate(across):
        copy.wait_recv()
        everyone, here = both[i % 2][1], thirds[i // 2]
        across_pair.append(send(everyone.at[4, here], everyone.at[5, here], (sibling, head)))
    for copy, _ in slabs:
        copy.wait_recv()
    for copy in across_pair:
        copy.wait_recv()
    for copy in list(near.values()) + pair + fresh + fresh_pair + across + near_pair + across_pair:
        copy.wait_send()
    for copy in [ask, peaks]:
        copy.wait_send()
    for copy, _ in slabs:
        copy.wait_send()
    for copy in own + late:
        copy.wait()


def gather(lists, positions, hidden, w_query, w_key, w_value, w_out, keys, values, x_count, z_count):
    held = keys.shape[0]
    tokens, depth = hidden.shape
    q_cols = w_query.shape[1]
    columns = w_out.shape[1] // (2 * z_count)
    anywhere = pl.BlockSpec(memory_space=pl.ANY)
    vmem = pl.BlockSpec(memory_space=pltpu.VMEM)
    steps = 5
    copies = 64
    state = jax.ShapeDtypeStruct((G, 2 * tokens, W), F32)
    return pl.pallas_call(
        functools.partial(gather_kernel, x_count, z_count, float(held * PAGE * x_count * 4)),
        out_shape=[
            jax.ShapeDtypeStruct((2 * x_count, held, PAGE, W), BF16),
            jax.ShapeDtypeStruct((2 * x_count, held, PAGE, W), BF16),
            jax.ShapeDtypeStruct((2 * tokens, q_cols), BF16),
            jax.ShapeDtypeStruct((2 * z_count, w_out.shape[0], columns), BF16),
            state,
            state,
            state,
        ],
        in_specs=[pl.BlockSpec(memory_space=pltpu.SMEM), vmem] + [anywhere] * 7,
        out_specs=[anywhere] * 4 + [vmem] * 3,
        scratch_shapes=[
            pltpu.VMEM((tokens, depth), BF16),
            pltpu.VMEM((depth, q_cols), BF16),
            pltpu.VMEM((depth, W), BF16),
            pltpu.VMEM((depth, W), BF16),
            pltpu.VMEM((tokens, q_cols + 2 * W), F32),
            pltpu.VMEM((2 * tokens, q_cols), BF16),
            pltpu.VMEM((tokens, 2 * W), BF16),
            pltpu.VMEM((2 * x_count, tokens, 2 * W), BF16),
            pltpu.VMEM((2 * held, PAGE, W), BF16),
            pltpu.VMEM((2 * held, PAGE, W), BF16),
            pltpu.VMEM((4 * held, PAGE, W), BF16),
            pltpu.VMEM((4 * held, PAGE, W), BF16),
            pltpu.VMEM((x_count // 2, 2 * tokens, 4 * tokens), F32),
            pltpu.VMEM((8, 2 * tokens), F32),
            pltpu.VMEM((8, 2 * tokens), F32),
            pltpu.SemaphoreType.DMA((copies,)),
            pltpu.SemaphoreType.DMA((copies,)),
            pltpu.SemaphoreType.DMA((steps, 4)),
            pltpu.SemaphoreType.DMA((17,)),
        ],
        compiler_params=pltpu.CompilerParams(
            collective_id=0, has_side_effects=True, vmem_limit_bytes=60 * 2**20
        ),
    )(lists, positions, hidden, w_query, w_key, w_value, w_out, keys, values)


def extra_kernel(
    list_ref, q_any, k_any, v_any, acc_in, m_in, l_in, acc_any, m_any, l_any, q, k, v, acc, m, l, sem
):
    count = list_ref[3 * LIST + 2]

    @pl.when(count > REST)
    def _():
        pairs = [(q_any, q), (k_any, k), (v_any, v), (acc_any, acc), (m_any, m), (l_any, l)]
        copies = [pltpu.make_async_copy(a, b, sem.at[i]) for i, (a, b) in enumerate(pairs)]
        for copy in copies:
            copy.start()
        for copy in copies:
            copy.wait()

        def step(i, _):
            keys, values, row = some_pages(list_ref, 2, REST + i * 4, 4, count, k, v)
            for g in range(G):
                absorb(q, g, keys, values, lambda: row, acc, m, l)
            return 0

        lax.fori_loop(0, (count - REST + 3) // 4, step, 0)
        back = [pltpu.make_async_copy(b, a, sem.at[i]) for i, (a, b) in enumerate(pairs[3:])]
        for copy in back:
            copy.start()
        for copy in back:
            copy.wait()


def extra(lists, queries, keys, values, acc, m, l):
    anywhere = pl.BlockSpec(memory_space=pl.ANY)
    state = jax.ShapeDtypeStruct(acc.shape, F32)
    return pl.pallas_call(
        extra_kernel,
        out_shape=[state] * 3,
        in_specs=[pl.BlockSpec(memory_space=pltpu.SMEM)] + [anywhere] * 6,
        out_specs=[anywhere] * 3,
        input_output_aliases={4: 0, 5: 1, 6: 2},
        scratch_shapes=[
            pltpu.VMEM(queries.shape, BF16),
            pltpu.VMEM(keys.shape, BF16),
            pltpu.VMEM(values.shape, BF16),
            pltpu.VMEM(acc.shape, F32),
            pltpu.VMEM(acc.shape, F32),
            pltpu.VMEM(acc.shape, F32),
            pltpu.SemaphoreType.DMA((6,)),
        ],
        compiler_params=pltpu.CompilerParams(vmem_limit_bytes=60 * 2**20),
    )(lists, queries, keys, values, acc, m, l)


def finish_kernel(
    x_count,
    z_count,
    list_ref,
    q_any,
    k_any,
    v_any,
    acc_any,
    m_any,
    l_any,
    w_out_ref,
    slab_ref,
    out_ref,
    q_ref,
    k_ref,
    v_ref,
    acc_ref,
    m_ref,
    l_ref,
    acc_in,
    stats_out,
    stats_in,
    slab_vmem,
    heads,
    send_sem,
    recv_sem,
    load_sem,
):
    ctx, head, core, at = places(x_count)
    z, y_lo = head // 2, head % 2
    tokens = acc_in.shape[1]
    y_peer = at(dy=1)

    def head_at(dz, dl):
        return lax.rem(z + dz, z_count) * 2 + lax.rem(y_lo + dl, 2)

    above, below, beside = head_at(1, 0), head_at(z_count - 1, 0), head_at(0, 1)
    loads = [
        pltpu.make_async_copy(source, target, load_sem.at[i])
        for i, (source, target) in enumerate(
            [
                (q_any, q_ref),
                (k_any, k_ref),
                (v_any, v_ref),
                (acc_any, acc_ref),
                (m_any, m_ref),
                (l_any, l_ref),
            ]
        )
    ]
    columns = slab_ref.shape[2]
    half = slab_ref.shape[1] // 2
    my_half = pl.ds(pl.multiple_of(core * half, half), half)
    my_cols = pl.ds(pl.multiple_of(head * columns, columns), columns)
    others = [lax.rem(head + i, 2 * z_count) for i in range(1, 2 * z_count)]
    weights = [pltpu.make_async_copy(w_out_ref.at[:, my_cols], slab_vmem.at[head], load_sem.at[6])]
    for i, which in enumerate(others):
        weights.append(
            pltpu.make_async_copy(
                slab_ref.at[which, my_half], slab_vmem.at[which, my_half], load_sem.at[7 + i]
            )
        )
    for load in loads + weights:
        load.start()

    barrier = pltpu.get_barrier_semaphore()
    met = [(y_peer, head), (at(dc=1), head), (ctx, above), (ctx, below), (ctx, beside)]
    for device in met:
        pl.semaphore_signal(barrier, inc=1, device_id=device, device_id_type=MESH)
    pl.semaphore_wait(barrier, len(met))

    counter = [0]
    started = []

    def send(source, target, device):
        i = counter[0]
        counter[0] += 1
        copy = pltpu.make_async_remote_copy(
            src_ref=source,
            dst_ref=target,
            send_sem=send_sem.at[i],
            recv_sem=recv_sem.at[i],
            device_id=device,
            device_id_type=MESH,
        )
        copy.start()
        started.append(copy)
        return copy

    halves = [
        send(slab_ref.at[which, my_half], slab_vmem.at[which, my_half], (at(dc=1), head))
        for which in others
    ]
    rows_peer = pl.ds(tokens, tokens)
    lane_row = lax.broadcasted_iota(jnp.int32, (tokens, W), 1)
    for load in loads:
        load.wait()
    blocks = [
        some_pages(list_ref, 2, first, BLOCK, list_ref[3 * LIST + 2], k_ref, v_ref)
        for first in range(0, REST, BLOCK)
    ]
    stats_copies, parts = [], []

    def attend(g):
        for keys, values, row in blocks:
            absorb(q_ref, g, keys, values, lambda: row, acc_ref, m_ref, l_ref)
        l_ref[g] = jnp.broadcast_to(jnp.sum(l_ref[g], axis=1, keepdims=True), l_ref.shape[1:])
        stats_out[g] = jnp.where(lane_row == 0, m_ref[g, tokens:], l_ref[g, tokens:]).T[:8]
        stats_copies.append(send(stats_out.at[g], stats_in.at[g], (y_peer, head)))
        parts.append(send(acc_ref.at[g, rows_peer], acc_in.at[g], (y_peer, head)))

    def pass_on(who, g, device):
        return send(heads.at[who, g], heads.at[who, g], (ctx, device))

    def use(pieces, start):
        lhs = jnp.concatenate([heads[who, g] for who, g in pieces], axis=1)
        rhs = jnp.concatenate(
            [slab_vmem[who, g * W : (g + 1) * W, :] for who, g in pieces], axis=0
        )
        product = jnp.dot(lhs, rhs, preferred_element_type=F32)
        if start:
            out_ref[...] = product
        else:
            out_ref[...] += product

    up, down, side, up_side, down_side, two, two_side = ({} for _ in range(7))
    attend(0)
    for t in range(G + 3):
        ready = []
        g = t
        if g + 1 < G:
            attend(g + 1)
        if g < G:
            stats_copies[g].wait_recv()
            parts[g].wait_recv()
            m1, l1 = m_ref[g, :tokens], l_ref[g, :tokens]
            theirs = jnp.concatenate([stats_in[g]] * (W // 8), axis=0).T
            m2, l2 = theirs[:, 0:1], theirs[:, 1:2]
            m = jnp.maximum(m1, m2)
            a1, a2 = jnp.exp(m1 - m), jnp.exp(m2 - m)
            total = l1 * a1 + l2 * a2
            heads[head, g] = (acc_ref[g, :tokens] * (a1 / total) + acc_in[g] * (a2 / total)).astype(BF16)
            side[g] = pass_on(head, g, beside)
            up[g] = pass_on(head, g, above)
            down[g] = pass_on(head, g, below)
            ready.append((head, g))
        g = t - 1
        if 0 <= g < G:
            side[g].wait_recv()
            up_side[g] = pass_on(beside, g, above)
            down_side[g] = pass_on(beside, g, below)
            up[g].wait_recv()
            down[g].wait_recv()
            if g % 2 == 0:
                two[g] = pass_on(below, g, above)
            else:
                two[g] = pass_on(above, g, below)
            ready += [(beside, g), (below, g), (above, g)]
        g = t - 2
        if 0 <= g < G:
            up_side[g].wait_recv()
            down_side[g].wait_recv()
            if g % 2 == 1:
                two_side[g] = pass_on(head_at(z_count - 1, 1), g, above)
            else:
                two_side[g] = pass_on(head_at(1, 1), g, below)
            ready += [(head_at(z_count - 1, 1), g), (head_at(1, 1), g)]
        g = t - 3
        if 0 <= g < G:
            two[g].wait_recv()
            two_side[g].wait_recv()
            ready += [(head_at(2, 0), g), (head_at(2, 1), g)]
        if t == 0:
            for load in weights:
                load.wait()
        if t == 1:
            for copy in halves:
                copy.wait_recv()
        use(ready, t == 0)
    for copy in started:
        copy.wait_send()


def finish(lists, queries, keys, values, acc, m, l, w_out, slab, x_count, z_count):
    tokens = queries.shape[0] // 2
    anywhere = pl.BlockSpec(memory_space=pl.ANY)
    copies = G * 9 + 2 * z_count
    return pl.pallas_call(
        functools.partial(finish_kernel, x_count, z_count),
        out_shape=jax.ShapeDtypeStruct((tokens, slab.shape[2]), F32),
        in_specs=[pl.BlockSpec(memory_space=pltpu.SMEM)] + [anywhere] * 8,
        out_specs=pl.BlockSpec(memory_space=pltpu.VMEM),
        scratch_shapes=[
            pltpu.VMEM(queries.shape, BF16),
            pltpu.VMEM(keys.shape, BF16),
            pltpu.VMEM(values.shape, BF16),
            pltpu.VMEM(acc.shape, F32),
            pltpu.VMEM(acc.shape, F32),
            pltpu.VMEM(acc.shape, F32),
            pltpu.VMEM((G, tokens, W), F32),
            pltpu.VMEM((G, 8, tokens), F32),
            pltpu.VMEM((G, 8, tokens), F32),
            pltpu.VMEM(slab.shape, BF16),
            pltpu.VMEM((2 * z_count, G, tokens, W), BF16),
            pltpu.SemaphoreType.DMA((copies,)),
            pltpu.SemaphoreType.DMA((copies,)),
            pltpu.SemaphoreType.DMA((6 + 2 * z_count,)),
        ],
        compiler_params=pltpu.CompilerParams(
            collective_id=1, has_side_effects=True, vmem_limit_bytes=60 * 2**20
        ),
    )(lists, queries, keys, values, acc, m, l, w_out, slab)


def on_device(
    hidden,
    positions,
    w_query,
    key_matrix,
    value_matrix,
    w_out,
    stored_keys,
    stored_values,
    kept_pages,
    page_slot,
):
    tokens = hidden.shape[0]
    ctx_count, head_count = lax.axis_size("ctx"), lax.axis_size("head")
    x_count, z_count = ctx_count // 4, head_count // 2
    table = positions.reshape(-1, W)
    lists = page_lists(kept_pages, page_slot, x_count)
    keys, values, queries, slab, acc, m, l = gather(
        lists, table, hidden, w_query, key_matrix, value_matrix, w_out,
        stored_keys.reshape(-1, PAGE, W), stored_values.reshape(-1, PAGE, W),
        x_count, z_count,
    )
    keys, values = keys.reshape(-1, PAGE, W), values.reshape(-1, PAGE, W)
    acc, m, l = extra(lists, queries, keys, values, acc, m, l)
    return finish(lists, queries, keys, values, acc, m, l, w_out, slab, x_count, z_count)


def solution(mesh):
    placed = (
        P("ctx", None),
        P(),
        P(None, "head"),
        P(None, "head"),
        P(None, "head"),
        P("head", None),
        P("ctx", "head"),
        P("ctx", "head"),
        P(),
        P(),
    )
    return jax.shard_map(
        on_device, mesh=mesh, in_specs=placed, out_specs=P("ctx", "head"), check_vma=False
    )
```

```python
import functools
import math

import jax
import jax.numpy as jnp
from jax import lax
from jax.experimental import pallas as pl
from jax.experimental.pallas import tpu as pltpu
from jax.sharding import PartitionSpec as P

G = 5
W = 128
PAGE = 128
LOW = -1e30
MASKED = -3e38
BLOCK = 12
NEAR = 12
SIDE = 12
REST = 36
LIST = 128
PIECES = 3
MESH = pl.DeviceIdType.MESH
F32 = jnp.float32
BF16 = jnp.bfloat16


def places(x_count):
    ctx = lax.axis_index("ctx")
    head = lax.axis_index("head")
    x, y_hi, core = ctx // 4, (ctx // 2) % 2, ctx % 2

    def at(dx=0, dy=0, dc=0):
        return (lax.rem(x + dx, x_count) * 2 + lax.rem(y_hi + dy, 2)) * 2 + lax.rem(core + dc, 2)

    return ctx, head, core, at


def list_kernel(x_count, kept_ref, slot_ref, list_ref):
    ctx, head = lax.axis_index("ctx"), lax.axis_index("head")
    x, y_hi, core = ctx // 4, (ctx // 2) % 2, ctx % 2
    slots = slot_ref.shape[0]
    per_device = slots // (4 * x_count)
    inverse = -(-65536 // per_device)
    assert all(i * inverse >> 16 == i // per_device for i in range(slots))
    assert x_count & (x_count - 1) == 0

    for first, many in ((0, NEAR), (LIST, SIDE), (2 * LIST, kept_ref.shape[1] + 4)):
        for i in range(many):
            list_ref[first + i] = 0

    def note(i, counts):
        near, side, rest = counts
        slot = slot_ref[kept_ref[head, i]]
        where = (slot * inverse) >> 16
        dx = ((where >> 2) - x) & (x_count - 1)
        dc = (where ^ core) & 1
        ours = ((where >> 1) & 1) == y_hi
        to_near = ours & (dx == 0) & (near < NEAR)
        to_side = ours & ((dx & 1) == 1) & (side < SIDE)
        to_rest = ours & jnp.logical_not(to_near | to_side)
        spot = jnp.where(
            to_near, near, jnp.where(to_side, LIST + side, jnp.where(to_rest, 2 * LIST + rest, 4 * LIST - 1))
        )
        held = jnp.where(to_side, dx - 1, 2 * dx) + dc
        list_ref[spot] = held * per_device + slot - where * per_device
        return near + to_near.astype(jnp.int32), side + to_side.astype(jnp.int32), rest + to_rest.astype(jnp.int32)

    zero = jnp.int32(0)
    near, side, rest = lax.fori_loop(0, kept_ref.shape[1], note, (zero, zero, zero), unroll=8)
    list_ref[3 * LIST] = near
    list_ref[3 * LIST + 1] = side
    list_ref[3 * LIST + 2] = rest


def page_lists(kept, slots, x_count):
    smem = pl.BlockSpec(memory_space=pltpu.SMEM)
    return pl.pallas_call(
        functools.partial(list_kernel, x_count),
        out_shape=jax.ShapeDtypeStruct((4 * LIST,), jnp.int32),
        in_specs=[smem] * 2,
        out_specs=smem,
    )(kept, slots)


def some_pages(list_ref, group, first, many, limit, k_ref, v_ref):
    ks, vs = [], []
    for j in range(many):
        page = list_ref[group * LIST + first + j]
        ks.append(k_ref[page])
        vs.append(v_ref[page])
    lane = lax.broadcasted_iota(jnp.int32, (1, many * PAGE), 1) // PAGE
    row = jnp.where(lane + first < limit, 0.0, MASKED)
    return jnp.concatenate(ks, axis=0), jnp.concatenate(vs, axis=0), row


def score(q_ref, g, keys, bias, rows=slice(None)):
    q = q_ref[rows, g * W : (g + 1) * W]
    return lax.dot_general(q, keys, (((1,), (1,)), ((), ())), preferred_element_type=F32) + bias()


def wide(tile, keys):
    return jnp.concatenate([tile] * (keys.shape[0] // W), axis=1)


def weigh(s, m, values):
    p = jnp.exp(s - m)
    sums = sum(p[:, c * W : (c + 1) * W] for c in range(p.shape[1] // W))
    return sums, jnp.dot(p.astype(BF16), values, preferred_element_type=F32)


def absorb(q_ref, g, keys, values, bias, acc_ref, m_ref, l_ref):
    s = score(q_ref, g, keys, bias)
    m_old = m_ref[g]
    m_new = jnp.maximum(m_old, jnp.max(s, axis=1, keepdims=True))
    rescale = jnp.exp(m_old - m_new)
    sums, summed = weigh(s, wide(m_new, keys), values)
    l_ref[g] = l_ref[g] * rescale + sums
    acc_ref[g] = acc_ref[g] * rescale + summed
    m_ref[g] = m_new


def gather_kernel(
    x_count,
    z_count,
    scale_base,
    list_ref,
    positions_ref,
    hidden_ref,
    w_query_ref,
    w_key_ref,
    w_value_ref,
    w_out_ref,
    keys_ref,
    values_ref,
    all_keys,
    all_values,
    queries,
    w_slab,
    acc_ref,
    m_ref,
    l_ref,
    hidden_vmem,
    wq_vmem,
    wk_vmem,
    wv_vmem,
    acc_vmem,
    q_vmem,
    new_vmem,
    all_new,
    near_k,
    near_v,
    side_k,
    side_v,
    bias_ref,
    stats_out,
    stats_in,
    send_sem,
    recv_sem,
    load_sem,
    local_sem,
):
    ctx, head, core, at = places(x_count)
    z, y_lo = head // 2, head % 2
    tokens = hidden_ref.shape[0]
    half = w_out_ref.shape[0] // 2
    columns = w_slab.shape[2]
    depth = hidden_ref.shape[1]
    steps = load_sem.shape[0]
    cut = depth // steps

    right, left, far = at(dx=1), at(dx=x_count - 1), at(dx=2)
    sibling, y_peer = at(dc=1), at(dy=1)
    cross = (ctx // 4 * 2 + lax.rem((ctx // 2) % 2 + core, 2)) * 2 + core
    out_peers = []
    for dz in range(z_count):
        for dl in range(2):
            if dz or dl:
                other = lax.rem(z + dz, z_count) * 2 + lax.rem(y_lo + dl, 2)
                back = lax.rem(z + z_count - dz, z_count) * 2 + lax.rem(y_lo + dl, 2)
                out_peers.append((cross if dl else ctx, other, back))

    barrier = pltpu.get_barrier_semaphore()
    met = [(c, head) for c in (right, left, far, sibling, y_peer)]
    met += [(c, h) for c, h, _ in out_peers]
    for device in met:
        pl.semaphore_signal(barrier, inc=1, device_id=device, device_id_type=MESH)
    pl.semaphore_wait(barrier, len(met))

    counter = [0]

    def send(source, target, device):
        i = counter[0]
        counter[0] += 1
        copy = pltpu.make_async_remote_copy(
            src_ref=source,
            dst_ref=target,
            send_sem=send_sem.at[i],
            recv_sem=recv_sem.at[i],
            device_id=device,
            device_id_type=MESH,
        )
        copy.start()
        return copy

    last = 2 * (x_count - 1)
    both = ((keys_ref, all_keys), (values_ref, all_values))
    thirds = [pl.ds(i * (keys_ref.shape[0] // PIECES), keys_ref.shape[0] // PIECES) for i in range(PIECES)]
    near = {}

    def send_near(i):
        for which, (mine, everyone) in enumerate(both):
            for slot, device in ((last, right), (2, left)):
                near[which, slot, i] = send(
                    mine.at[thirds[i]], everyone.at[slot, thirds[i]], (device, head)
                )

    send_near(0)
    my_half = pl.ds(pl.multiple_of(core * half, half), half)
    slabs = []

    def send_slabs(many):
        for c, h, _ in out_peers[len(slabs) : len(slabs) + many]:
            cols = pl.ds(pl.multiple_of(h * columns, columns), columns)
            slabs.append(send(w_out_ref.at[my_half, cols], w_slab.at[head, my_half], (c, h)))

    send_slabs(2)
    pair = [send(mine, everyone.at[1], (sibling, head)) for mine, everyone in both]
    loads = []
    for i in range(steps):
        rows = pl.ds(i * cut, cut)
        pieces = [
            pltpu.make_async_copy(hidden_ref.at[:, rows], hidden_vmem.at[:, rows], load_sem.at[i, 0]),
            pltpu.make_async_copy(w_query_ref.at[rows], wq_vmem.at[rows], load_sem.at[i, 1]),
            pltpu.make_async_copy(w_key_ref.at[rows], wk_vmem.at[rows], load_sem.at[i, 2]),
            pltpu.make_async_copy(w_value_ref.at[rows], wv_vmem.at[rows], load_sem.at[i, 3]),
        ]
        for piece in pieces:
            piece.start()
        loads.append(pieces)
    keep = keys_ref.shape[0]
    near_loads = [
        pltpu.make_async_copy(keys_ref, near_k.at[pl.ds(0, keep)], local_sem.at[5]),
        pltpu.make_async_copy(values_ref, near_v.at[pl.ds(0, keep)], local_sem.at[6]),
    ]
    for copy in near_loads:
        copy.start()

    q_cols = wq_vmem.shape[1]
    def project(pieces, parts):
        for i in range(steps):
            for piece in pieces:
                loads[i][piece].wait()
            rows = slice(i * cut, (i + 1) * cut)
            part = hidden_vmem[:, rows]
            for w_ref, first, end in parts:
                product = jnp.dot(part, w_ref[rows, :], preferred_element_type=F32)
                if i:
                    acc_vmem[:, first:end] += product
                else:
                    acc_vmem[:, first:end] = product

    project((0, 1), ((wq_vmem, 0, q_cols),))

    def position_row(which):
        lines = [positions_ref[pl.ds(which * (tokens // W) + i, 1), :] for i in range(tokens // W)]
        return jnp.concatenate(lines, axis=1)

    my_positions = position_row(ctx)
    spread = jnp.broadcast_to(my_positions, (tokens, tokens))
    diagonal = lax.broadcasted_iota(jnp.int32, (tokens, tokens), 0) == lax.broadcasted_iota(
        jnp.int32, (tokens, tokens), 1
    )
    column = jnp.sum(jnp.where(diagonal, spread, 0).astype(F32), axis=1, keepdims=True)
    thousands = jnp.floor((column + (scale_base + 1.0)) * (1.0 / 8192.0))
    scaling = (jnp.log(thousands + 1.0) * 0.1 + 1.0) / math.sqrt(W)
    q_vmem[:tokens, :] = (acc_vmem[:, :q_cols] * scaling).astype(BF16)
    rows_own, rows_peer = pl.ds(0, tokens), pl.ds(tokens, tokens)
    ask = send(q_vmem.at[rows_own], q_vmem.at[rows_peer], (y_peer, head))
    project((2, 3), ((wk_vmem, q_cols, q_cols + W), (wv_vmem, q_cols + W, q_cols + 2 * W)))
    new_vmem[...] = acc_vmem[:, q_cols:].astype(BF16)
    fresh = [
        send(new_vmem, all_new.at[last], (right, head)),
        send(new_vmem, all_new.at[2], (left, head)),
        send(new_vmem, all_new.at[4], (far, head)),
    ]
    fresh_pair = [send(new_vmem, all_new.at[1], (sibling, head))]
    all_new[0] = new_vmem[...]
    for i in range(1, PIECES):
        send_near(i)
    send_slabs(1)

    def positions_of(which):
        return position_row(which).astype(F32)

    def as_column(row):
        spread = jnp.where(diagonal, jnp.broadcast_to(row, (tokens, tokens)), 0.0)
        return jnp.sum(spread, axis=1, keepdims=True)

    mine = jnp.concatenate([column, as_column(positions_of(y_peer))], axis=0)
    for slot in range(2 * x_count):
        theirs = positions_of(at(dx=slot // 2, dc=slot % 2))
        bias_ref[slot // 4, :, (slot % 4) * tokens : (slot % 4 + 1) * tokens] = jnp.where(
            theirs > mine, MASKED, 0.0
        )

    for copy, everyone, held, sem in zip(pair[:2], (all_keys, all_values), (near_k, near_v), (7, 8)):
        copy.wait_recv()
        load = pltpu.make_async_copy(everyone.at[1], held.at[pl.ds(keep, keep)], local_sem.at[sem])
        load.start()
        near_loads.append(load)
    for load in near_loads:
        load.wait()
    own = [
        pltpu.make_async_copy(held.at[pl.ds(0, keep)], everyone.at[0], local_sem.at[i])
        for i, (held, everyone) in enumerate(((near_k, all_keys), (near_v, all_values)))
    ]
    for copy in own:
        copy.start()

    near_args = (list_ref, 0, 0, NEAR, list_ref[3 * LIST], near_k, near_v)

    def new_block(b):
        pieces = [all_new[4 * b + j] for j in range(4)]
        block = jnp.concatenate(pieces, axis=0)
        return block[:, :W], block[:, W:], lambda: bias_ref[b]

    def peaks_of(rows):
        here = slice(rows * tokens, (rows + 1) * tokens)
        keys, _, row = some_pages(*near_args)
        for g in range(G):
            s = score(q_vmem, g, keys, lambda: row, here)
            m_ref[g, here] = jnp.maximum(
                jnp.max(s, axis=1, keepdims=True), jnp.full((tokens, W), LOW, F32)
            )
        if rows == 0:
            for copy, slot in zip(fresh, (last, 2, 4)):
                copy.wait_recv()
                fresh_pair.append(send(all_new.at[slot], all_new.at[slot + 1], (sibling, head)))
            for copy in fresh_pair:
                copy.wait_recv()

        def new_peak(b, _):
            keys, _, _ = new_block(b)
            for g in range(G):
                s = score(q_vmem, g, keys, lambda: bias_ref[b, here], here)
                m_ref[g, here] = jnp.maximum(m_ref[g, here], jnp.max(s, axis=1, keepdims=True))
            return 0

        lax.fori_loop(0, x_count // 2, new_peak, 0)

    peaks_of(0)
    send_slabs(1)
    ask.wait_recv()
    late = [pltpu.make_async_copy(q_vmem, queries, local_sem.at[3])]
    late[0].start()
    peaks_of(1)
    lane = lax.broadcasted_iota(jnp.int32, (2 * tokens, W), 1)
    stats = jnp.zeros((2 * tokens, W), F32)
    for g in range(G):
        stats = jnp.where(lane == g, m_ref[g], stats)
    stats_out[...] = stats.T[:8]
    peaks = send(stats_out, stats_in, (y_peer, head))

    across, near_pair, side_loads = [], [], []

    def pass_on(i):
        for which, (_, everyone) in enumerate(both):
            for slot in (last, 2):
                near[which, slot, i].wait_recv()
                here = everyone.at[slot, thirds[i]]
                if which == 0 and slot == last:
                    across.append(send(here, everyone.at[4, thirds[i]], (right, head)))
                if which == 1 and slot == 2:
                    across.append(send(here, everyone.at[4, thirds[i]], (left, head)))
                near_pair.append(send(here, everyone.at[slot + 1, thirds[i]], (sibling, head)))

    pass_on(0)
    send_slabs(1)
    peaks.wait_recv()
    their_peaks = jnp.concatenate([stats_in[...]] * (W // 8), axis=0).T
    for g in range(G):
        theirs = their_peaks[:, g : g + 1]
        theirs = jnp.concatenate([theirs[tokens:], theirs[:tokens]], axis=0)
        m_ref[g] = jnp.maximum(m_ref[g], theirs)

    keys, values, row = some_pages(*near_args)
    for g in range(G):
        l_ref[g], acc_ref[g] = weigh(score(q_vmem, g, keys, lambda: row), wide(m_ref[g], keys), values)

    for i in range(1, PIECES):
        pass_on(i)
    send_slabs(len(out_peers))

    def hold(odd):
        for which, (_, everyone) in enumerate(both):
            for spot, slot in ((0, 2), (2, last)):
                load = pltpu.make_async_copy(
                    everyone.at[slot + odd],
                    (side_k, side_v)[which].at[pl.ds((spot + odd) * keep, keep)],
                    local_sem.at[9 + len(side_loads)],
                )
                load.start()
                side_loads.append(load)

    hold(0)

    def new_weights(b, _):
        keys, values, bias = new_block(b)
        for g in range(G):
            sums, summed = weigh(score(q_vmem, g, keys, bias), wide(m_ref[g], keys), values)
            l_ref[g] += sums
            acc_ref[g] += summed
        return 0

    lax.fori_loop(0, x_count // 2, new_weights, 0)

    for copy in near_pair:
        copy.wait_recv()
    hold(1)
    for load in side_loads:
        load.wait()
    keys, values, row = some_pages(list_ref, 1, 0, SIDE, list_ref[3 * LIST + 1], side_k, side_v)
    for g in range(G):
        absorb(q_vmem, g, keys, values, lambda: row, acc_ref, m_ref, l_ref)

    across_pair = []
    for i, copy in enumerate(across):
        copy.wait_recv()
        everyone, here = both[i % 2][1], thirds[i // 2]
        across_pair.append(send(everyone.at[4, here], everyone.at[5, here], (sibling, head)))
    for copy in slabs:
        copy.wait_recv()
    for copy in across_pair:
        copy.wait_recv()
    for copy in list(near.values()) + pair + fresh + fresh_pair + across + near_pair + across_pair:
        copy.wait_send()
    for copy in [ask, peaks]:
        copy.wait_send()
    for copy in slabs:
        copy.wait_send()
    for copy in own + late:
        copy.wait()


def gather(lists, positions, hidden, w_query, w_key, w_value, w_out, keys, values, x_count, z_count):
    held = keys.shape[0]
    tokens, depth = hidden.shape
    q_cols = w_query.shape[1]
    columns = w_out.shape[1] // (2 * z_count)
    anywhere = pl.BlockSpec(memory_space=pl.ANY)
    vmem = pl.BlockSpec(memory_space=pltpu.VMEM)
    steps = 5
    copies = 64
    state = jax.ShapeDtypeStruct((G, 2 * tokens, W), F32)
    return pl.pallas_call(
        functools.partial(gather_kernel, x_count, z_count, float(held * PAGE * x_count * 4)),
        out_shape=[
            jax.ShapeDtypeStruct((2 * x_count, held, PAGE, W), BF16),
            jax.ShapeDtypeStruct((2 * x_count, held, PAGE, W), BF16),
            jax.ShapeDtypeStruct((2 * tokens, q_cols), BF16),
            jax.ShapeDtypeStruct((2 * z_count, w_out.shape[0], columns), BF16),
            state,
            state,
            state,
        ],
        in_specs=[pl.BlockSpec(memory_space=pltpu.SMEM), vmem] + [anywhere] * 7,
        out_specs=[anywhere] * 4 + [vmem] * 3,
        scratch_shapes=[
            pltpu.VMEM((tokens, depth), BF16),
            pltpu.VMEM((depth, q_cols), BF16),
            pltpu.VMEM((depth, W), BF16),
            pltpu.VMEM((depth, W), BF16),
            pltpu.VMEM((tokens, q_cols + 2 * W), F32),
            pltpu.VMEM((2 * tokens, q_cols), BF16),
            pltpu.VMEM((tokens, 2 * W), BF16),
            pltpu.VMEM((2 * x_count, tokens, 2 * W), BF16),
            pltpu.VMEM((2 * held, PAGE, W), BF16),
            pltpu.VMEM((2 * held, PAGE, W), BF16),
            pltpu.VMEM((4 * held, PAGE, W), BF16),
            pltpu.VMEM((4 * held, PAGE, W), BF16),
            pltpu.VMEM((x_count // 2, 2 * tokens, 4 * tokens), F32),
            pltpu.VMEM((8, 2 * tokens), F32),
            pltpu.VMEM((8, 2 * tokens), F32),
            pltpu.SemaphoreType.DMA((copies,)),
            pltpu.SemaphoreType.DMA((copies,)),
            pltpu.SemaphoreType.DMA((steps, 4)),
            pltpu.SemaphoreType.DMA((17,)),
        ],
        compiler_params=pltpu.CompilerParams(
            collective_id=0, has_side_effects=True, vmem_limit_bytes=60 * 2**20
        ),
    )(lists, positions, hidden, w_query, w_key, w_value, w_out, keys, values)


def extra_kernel(
    list_ref, q_any, k_any, v_any, acc_in, m_in, l_in, acc_any, m_any, l_any, q, k, v, acc, m, l, sem
):
    count = list_ref[3 * LIST + 2]

    @pl.when(count > REST)
    def _():
        pairs = [(q_any, q), (k_any, k), (v_any, v), (acc_any, acc), (m_any, m), (l_any, l)]
        copies = [pltpu.make_async_copy(a, b, sem.at[i]) for i, (a, b) in enumerate(pairs)]
        for copy in copies:
            copy.start()
        for copy in copies:
            copy.wait()

        def step(i, _):
            keys, values, row = some_pages(list_ref, 2, REST + i * 4, 4, count, k, v)
            for g in range(G):
                absorb(q, g, keys, values, lambda: row, acc, m, l)
            return 0

        lax.fori_loop(0, (count - REST + 3) // 4, step, 0)
        back = [pltpu.make_async_copy(b, a, sem.at[i]) for i, (a, b) in enumerate(pairs[3:])]
        for copy in back:
            copy.start()
        for copy in back:
            copy.wait()


def extra(lists, queries, keys, values, acc, m, l):
    anywhere = pl.BlockSpec(memory_space=pl.ANY)
    state = jax.ShapeDtypeStruct(acc.shape, F32)
    return pl.pallas_call(
        extra_kernel,
        out_shape=[state] * 3,
        in_specs=[pl.BlockSpec(memory_space=pltpu.SMEM)] + [anywhere] * 6,
        out_specs=[anywhere] * 3,
        input_output_aliases={4: 0, 5: 1, 6: 2},
        scratch_shapes=[
            pltpu.VMEM(queries.shape, BF16),
            pltpu.VMEM(keys.shape, BF16),
            pltpu.VMEM(values.shape, BF16),
            pltpu.VMEM(acc.shape, F32),
            pltpu.VMEM(acc.shape, F32),
            pltpu.VMEM(acc.shape, F32),
            pltpu.SemaphoreType.DMA((6,)),
        ],
        compiler_params=pltpu.CompilerParams(vmem_limit_bytes=60 * 2**20),
    )(lists, queries, keys, values, acc, m, l)


def finish_kernel(
    x_count,
    z_count,
    list_ref,
    q_any,
    k_any,
    v_any,
    acc_any,
    m_any,
    l_any,
    w_out_ref,
    slab_ref,
    out_ref,
    q_ref,
    k_ref,
    v_ref,
    acc_ref,
    m_ref,
    l_ref,
    acc_in,
    stats_out,
    stats_in,
    slab_vmem,
    heads,
    send_sem,
    recv_sem,
    load_sem,
):
    ctx, head, core, at = places(x_count)
    z, y_lo = head // 2, head % 2
    tokens = acc_in.shape[1]
    y_peer = at(dy=1)

    def head_at(dz, dl):
        return lax.rem(z + dz, z_count) * 2 + lax.rem(y_lo + dl, 2)

    above, below, beside = head_at(1, 0), head_at(z_count - 1, 0), head_at(0, 1)
    loads = [
        pltpu.make_async_copy(source, target, load_sem.at[i])
        for i, (source, target) in enumerate(
            [
                (q_any, q_ref),
                (k_any, k_ref),
                (v_any, v_ref),
                (acc_any, acc_ref),
                (m_any, m_ref),
                (l_any, l_ref),
            ]
        )
    ]
    columns = slab_ref.shape[2]
    half = slab_ref.shape[1] // 2
    my_half = pl.ds(pl.multiple_of(core * half, half), half)
    my_cols = pl.ds(pl.multiple_of(head * columns, columns), columns)
    others = [lax.rem(head + i, 2 * z_count) for i in range(1, 2 * z_count)]
    weights = [pltpu.make_async_copy(w_out_ref.at[:, my_cols], slab_vmem.at[head], load_sem.at[6])]
    for i, which in enumerate(others):
        weights.append(
            pltpu.make_async_copy(
                slab_ref.at[which, my_half], slab_vmem.at[which, my_half], load_sem.at[7 + i]
            )
        )
    for load in loads + weights:
        load.start()

    barrier = pltpu.get_barrier_semaphore()
    met = [(y_peer, head), (at(dc=1), head), (ctx, above), (ctx, below), (ctx, beside)]
    for device in met:
        pl.semaphore_signal(barrier, inc=1, device_id=device, device_id_type=MESH)
    pl.semaphore_wait(barrier, len(met))

    counter = [0]
    started = []

    def send(source, target, device):
        i = counter[0]
        counter[0] += 1
        copy = pltpu.make_async_remote_copy(
            src_ref=source,
            dst_ref=target,
            send_sem=send_sem.at[i],
            recv_sem=recv_sem.at[i],
            device_id=device,
            device_id_type=MESH,
        )
        copy.start()
        started.append(copy)
        return copy

    halves = [
        send(slab_ref.at[which, my_half], slab_vmem.at[which, my_half], (at(dc=1), head))
        for which in others
    ]
    rows_peer = pl.ds(tokens, tokens)
    lane_row = lax.broadcasted_iota(jnp.int32, (tokens, W), 1)
    for load in loads:
        load.wait()
    blocks = [
        some_pages(list_ref, 2, first, BLOCK, list_ref[3 * LIST + 2], k_ref, v_ref)
        for first in range(0, REST, BLOCK)
    ]
    stats_copies, parts = [], []

    def attend(g):
        for keys, values, row in blocks:
            absorb(q_ref, g, keys, values, lambda: row, acc_ref, m_ref, l_ref)
        l_ref[g] = jnp.broadcast_to(jnp.sum(l_ref[g], axis=1, keepdims=True), l_ref.shape[1:])
        stats_out[g] = jnp.where(lane_row == 0, m_ref[g, tokens:], l_ref[g, tokens:]).T[:8]
        stats_copies.append(send(stats_out.at[g], stats_in.at[g], (y_peer, head)))
        parts.append(send(acc_ref.at[g, rows_peer], acc_in.at[g], (y_peer, head)))

    def pass_on(who, g, device):
        return send(heads.at[who, g], heads.at[who, g], (ctx, device))

    def use(pieces, start):
        lhs = jnp.concatenate([heads[who, g] for who, g in pieces], axis=1)
        rhs = jnp.concatenate(
            [slab_vmem[who, g * W : (g + 1) * W, :] for who, g in pieces], axis=0
        )
        product = jnp.dot(lhs, rhs, preferred_element_type=F32)
        if start:
            out_ref[...] = product
        else:
            out_ref[...] += product

    up, down, side, up_side, down_side, two, two_side = ({} for _ in range(7))
    attend(0)
    for t in range(G + 3):
        ready = []
        g = t
        if g + 1 < G:
            attend(g + 1)
        if g < G:
            stats_copies[g].wait_recv()
            parts[g].wait_recv()
            m1, l1 = m_ref[g, :tokens], l_ref[g, :tokens]
            theirs = jnp.concatenate([stats_in[g]] * (W // 8), axis=0).T
            m2, l2 = theirs[:, 0:1], theirs[:, 1:2]
            m = jnp.maximum(m1, m2)
            a1, a2 = jnp.exp(m1 - m), jnp.exp(m2 - m)
            total = l1 * a1 + l2 * a2
            heads[head, g] = (acc_ref[g, :tokens] * (a1 / total) + acc_in[g] * (a2 / total)).astype(BF16)
            side[g] = pass_on(head, g, beside)
            up[g] = pass_on(head, g, above)
            down[g] = pass_on(head, g, below)
            ready.append((head, g))
        g = t - 1
        if 0 <= g < G:
            side[g].wait_recv()
            up_side[g] = pass_on(beside, g, above)
            down_side[g] = pass_on(beside, g, below)
            up[g].wait_recv()
            down[g].wait_recv()
            if g % 2 == 0:
                two[g] = pass_on(below, g, above)
            else:
                two[g] = pass_on(above, g, below)
            ready += [(beside, g), (below, g), (above, g)]
        g = t - 2
        if 0 <= g < G:
            up_side[g].wait_recv()
            down_side[g].wait_recv()
            if g % 2 == 1:
                two_side[g] = pass_on(head_at(z_count - 1, 1), g, above)
            else:
                two_side[g] = pass_on(head_at(1, 1), g, below)
            ready += [(head_at(z_count - 1, 1), g), (head_at(1, 1), g)]
        g = t - 3
        if 0 <= g < G:
            two[g].wait_recv()
            two_side[g].wait_recv()
            ready += [(head_at(2, 0), g), (head_at(2, 1), g)]
        if t == 0:
            for load in weights:
                load.wait()
        if t == 1:
            for copy in halves:
                copy.wait_recv()
        use(ready, t == 0)
    for copy in started:
        copy.wait_send()


def finish(lists, queries, keys, values, acc, m, l, w_out, slab, x_count, z_count):
    tokens = queries.shape[0] // 2
    anywhere = pl.BlockSpec(memory_space=pl.ANY)
    copies = G * 9 + 2 * z_count
    return pl.pallas_call(
        functools.partial(finish_kernel, x_count, z_count),
        out_shape=jax.ShapeDtypeStruct((tokens, slab.shape[2]), F32),
        in_specs=[pl.BlockSpec(memory_space=pltpu.SMEM)] + [anywhere] * 8,
        out_specs=pl.BlockSpec(memory_space=pltpu.VMEM),
        scratch_shapes=[
            pltpu.VMEM(queries.shape, BF16),
            pltpu.VMEM(keys.shape, BF16),
            pltpu.VMEM(values.shape, BF16),
            pltpu.VMEM(acc.shape, F32),
            pltpu.VMEM(acc.shape, F32),
            pltpu.VMEM(acc.shape, F32),
            pltpu.VMEM((G, tokens, W), F32),
            pltpu.VMEM((G, 8, tokens), F32),
            pltpu.VMEM((G, 8, tokens), F32),
            pltpu.VMEM(slab.shape, BF16),
            pltpu.VMEM((2 * z_count, G, tokens, W), BF16),
            pltpu.SemaphoreType.DMA((copies,)),
            pltpu.SemaphoreType.DMA((copies,)),
            pltpu.SemaphoreType.DMA((6 + 2 * z_count,)),
        ],
        compiler_params=pltpu.CompilerParams(
            collective_id=1, has_side_effects=True, vmem_limit_bytes=60 * 2**20
        ),
    )(lists, queries, keys, values, acc, m, l, w_out, slab)


def on_device(
    hidden,
    positions,
    w_query,
    key_matrix,
    value_matrix,
    w_out,
    stored_keys,
    stored_values,
    kept_pages,
    page_slot,
):
    tokens = hidden.shape[0]
    ctx_count, head_count = lax.axis_size("ctx"), lax.axis_size("head")
    x_count, z_count = ctx_count // 4, head_count // 2
    table = positions.reshape(-1, W)
    lists = page_lists(kept_pages, page_slot, x_count)
    keys, values, queries, slab, acc, m, l = gather(
        lists, table, hidden, w_query, key_matrix, value_matrix, w_out,
        stored_keys.reshape(-1, PAGE, W), stored_values.reshape(-1, PAGE, W),
        x_count, z_count,
    )
    keys, values = keys.reshape(-1, PAGE, W), values.reshape(-1, PAGE, W)
    acc, m, l = extra(lists, queries, keys, values, acc, m, l)
    return finish(lists, queries, keys, values, acc, m, l, w_out, slab, x_count, z_count)


def solution(mesh):
    placed = (
        P("ctx", None),
        P(),
        P(None, "head"),
        P(None, "head"),
        P(None, "head"),
        P("head", None),
        P("ctx", "head"),
        P("ctx", "head"),
        P(),
        P(),
    )
    return jax.shard_map(
        on_device, mesh=mesh, in_specs=placed, out_specs=P("ctx", "head"), check_vma=False
    )
```

```python
import functools
import math

import jax
import jax.numpy as jnp
from jax import lax
from jax.experimental import pallas as pl
from jax.experimental.pallas import tpu as pltpu
from jax.sharding import PartitionSpec as P

G = 5
W = 128
PAGE = 128
LOW = -1e30
MASKED = -3e38
BLOCK = 12
NEAR = 12
SIDE = 12
REST = 36
LIST = 128
PIECES = 3
MESH = pl.DeviceIdType.MESH
F32 = jnp.float32
BF16 = jnp.bfloat16


def places(x_count):
    ctx = lax.axis_index("ctx")
    head = lax.axis_index("head")
    x, y_hi, core = ctx // 4, (ctx // 2) % 2, ctx % 2

    def at(dx=0, dy=0, dc=0):
        return (lax.rem(x + dx, x_count) * 2 + lax.rem(y_hi + dy, 2)) * 2 + lax.rem(core + dc, 2)

    return ctx, head, core, at


def list_kernel(x_count, kept_ref, slot_ref, list_ref):
    ctx, head = lax.axis_index("ctx"), lax.axis_index("head")
    x, y_hi, core = ctx // 4, (ctx // 2) % 2, ctx % 2
    slots = slot_ref.shape[0]
    per_device = slots // (4 * x_count)
    inverse = -(-65536 // per_device)
    assert all(i * inverse >> 16 == i // per_device for i in range(slots))
    assert x_count & (x_count - 1) == 0

    for first, many in ((0, NEAR), (LIST, SIDE), (2 * LIST, kept_ref.shape[1] + 4)):
        for i in range(many):
            list_ref[first + i] = 0

    def note(i, counts):
        near, side, rest = counts
        slot = slot_ref[kept_ref[head, i]]
        where = (slot * inverse) >> 16
        dx = ((where >> 2) - x) & (x_count - 1)
        dc = (where ^ core) & 1
        ours = ((where >> 1) & 1) == y_hi
        to_near = ours & (dx == 0) & (near < NEAR)
        to_side = ours & ((dx & 1) == 1) & (side < SIDE)
        to_rest = ours & jnp.logical_not(to_near | to_side)
        spot = jnp.where(
            to_near, near, jnp.where(to_side, LIST + side, jnp.where(to_rest, 2 * LIST + rest, 4 * LIST - 1))
        )
        held = jnp.where(to_side, dx - 1, 2 * dx) + dc
        list_ref[spot] = held * per_device + slot - where * per_device
        return near + to_near.astype(jnp.int32), side + to_side.astype(jnp.int32), rest + to_rest.astype(jnp.int32)

    zero = jnp.int32(0)
    near, side, rest = lax.fori_loop(0, kept_ref.shape[1], note, (zero, zero, zero), unroll=8)
    list_ref[3 * LIST] = near
    list_ref[3 * LIST + 1] = side
    list_ref[3 * LIST + 2] = rest


def page_lists(kept, slots, x_count):
    smem = pl.BlockSpec(memory_space=pltpu.SMEM)
    return pl.pallas_call(
        functools.partial(list_kernel, x_count),
        out_shape=jax.ShapeDtypeStruct((4 * LIST,), jnp.int32),
        in_specs=[smem] * 2,
        out_specs=smem,
    )(kept, slots)


def some_pages(list_ref, group, first, many, limit, k_ref, v_ref):
    ks, vs = [], []
    for j in range(many):
        page = list_ref[group * LIST + first + j]
        ks.append(k_ref[page])
        vs.append(v_ref[page])
    lane = lax.broadcasted_iota(jnp.int32, (1, many * PAGE), 1) // PAGE
    row = jnp.where(lane + first < limit, 0.0, MASKED)
    return jnp.concatenate(ks, axis=0), jnp.concatenate(vs, axis=0), row


def score(q_ref, g, keys, bias, rows=slice(None)):
    q = q_ref[rows, g * W : (g + 1) * W]
    return lax.dot_general(q, keys, (((1,), (1,)), ((), ())), preferred_element_type=F32) + bias()


def wide(tile, keys):
    return jnp.concatenate([tile] * (keys.shape[0] // W), axis=1)


def weigh(s, m, values):
    p = jnp.exp(s - m)
    sums = sum(p[:, c * W : (c + 1) * W] for c in range(p.shape[1] // W))
    return sums, jnp.dot(p.astype(BF16), values, preferred_element_type=F32)


def absorb(q_ref, g, keys, values, bias, acc_ref, m_ref, l_ref):
    s = score(q_ref, g, keys, bias)
    m_old = m_ref[g]
    m_new = jnp.maximum(m_old, jnp.max(s, axis=1, keepdims=True))
    rescale = jnp.exp(m_old - m_new)
    sums, summed = weigh(s, wide(m_new, keys), values)
    l_ref[g] = l_ref[g] * rescale + sums
    acc_ref[g] = acc_ref[g] * rescale + summed
    m_ref[g] = m_new


def gather_kernel(
    x_count,
    z_count,
    scale_base,
    list_ref,
    positions_ref,
    hidden_ref,
    w_query_ref,
    w_key_ref,
    w_value_ref,
    w_out_ref,
    keys_ref,
    values_ref,
    all_keys,
    all_values,
    queries,
    w_slab,
    acc_ref,
    m_ref,
    l_ref,
    hidden_vmem,
    wq_vmem,
    wk_vmem,
    wv_vmem,
    acc_vmem,
    q_vmem,
    new_vmem,
    all_new,
    near_k,
    near_v,
    side_k,
    side_v,
    bias_ref,
    stats_out,
    stats_in,
    send_sem,
    recv_sem,
    load_sem,
    local_sem,
):
    ctx, head, core, at = places(x_count)
    z, y_lo = head // 2, head % 2
    tokens = hidden_ref.shape[0]
    half = w_out_ref.shape[0] // 2
    columns = w_slab.shape[2]
    depth = hidden_ref.shape[1]
    steps = load_sem.shape[0]
    cut = depth // steps

    right, left, far = at(dx=1), at(dx=x_count - 1), at(dx=2)
    sibling, y_peer = at(dc=1), at(dy=1)
    cross = (ctx // 4 * 2 + lax.rem((ctx // 2) % 2 + core, 2)) * 2 + core
    out_peers = []
    order = [(0, 1)] + [(dz, dl) for dz in range(2, z_count - 1) for dl in range(2)]
    order += [(dz, dl) for dl in range(2) for dz in (1, z_count - 1)]
    for dz, dl in order:
        other = lax.rem(z + dz, z_count) * 2 + lax.rem(y_lo + dl, 2)
        back = lax.rem(z + z_count - dz, z_count) * 2 + lax.rem(y_lo + dl, 2)
        out_peers.append((cross if dl else ctx, other, back))

    barrier = pltpu.get_barrier_semaphore()
    met = [(c, head) for c in (right, left, far, sibling, y_peer)]
    met += [(c, h) for c, h, _ in out_peers]
    for device in met:
        pl.semaphore_signal(barrier, inc=1, device_id=device, device_id_type=MESH)
    pl.semaphore_wait(barrier, len(met))

    counter = [0]

    def send(source, target, device):
        i = counter[0]
        counter[0] += 1
        copy = pltpu.make_async_remote_copy(
            src_ref=source,
            dst_ref=target,
            send_sem=send_sem.at[i],
            recv_sem=recv_sem.at[i],
            device_id=device,
            device_id_type=MESH,
        )
        copy.start()
        return copy

    last = 2 * (x_count - 1)
    both = ((keys_ref, all_keys), (values_ref, all_values))
    thirds = [pl.ds(i * (keys_ref.shape[0] // PIECES), keys_ref.shape[0] // PIECES) for i in range(PIECES)]
    near = {}

    def send_near(i):
        for which, (mine, everyone) in enumerate(both):
            for slot, device in ((last, right), (2, left)):
                near[which, slot, i] = send(
                    mine.at[thirds[i]], everyone.at[slot, thirds[i]], (device, head)
                )

    send_near(0)
    my_half = pl.ds(pl.multiple_of(core * half, half), half)
    slabs = []

    def send_slabs(many):
        for c, h, _ in out_peers[len(slabs) : len(slabs) + many]:
            cols = pl.ds(pl.multiple_of(h * columns, columns), columns)
            slabs.append(send(w_out_ref.at[my_half, cols], w_slab.at[head, my_half], (c, h)))

    send_slabs(2)
    pair = [send(mine, everyone.at[1], (sibling, head)) for mine, everyone in both]
    loads = []
    for i in range(steps):
        rows = pl.ds(i * cut, cut)
        pieces = [
            pltpu.make_async_copy(hidden_ref.at[:, rows], hidden_vmem.at[:, rows], load_sem.at[i, 0]),
            pltpu.make_async_copy(w_query_ref.at[rows], wq_vmem.at[rows], load_sem.at[i, 1]),
            pltpu.make_async_copy(w_key_ref.at[rows], wk_vmem.at[rows], load_sem.at[i, 2]),
            pltpu.make_async_copy(w_value_ref.at[rows], wv_vmem.at[rows], load_sem.at[i, 3]),
        ]
        for piece in pieces:
            piece.start()
        loads.append(pieces)
    keep = keys_ref.shape[0]
    near_loads = [
        pltpu.make_async_copy(keys_ref, near_k.at[pl.ds(0, keep)], local_sem.at[5]),
        pltpu.make_async_copy(values_ref, near_v.at[pl.ds(0, keep)], local_sem.at[6]),
    ]
    for copy in near_loads:
        copy.start()

    q_cols = wq_vmem.shape[1]
    def project(pieces, parts):
        for i in range(steps):
            for piece in pieces:
                loads[i][piece].wait()
            rows = slice(i * cut, (i + 1) * cut)
            part = hidden_vmem[:, rows]
            for w_ref, first, end in parts:
                product = jnp.dot(part, w_ref[rows, :], preferred_element_type=F32)
                if i:
                    acc_vmem[:, first:end] += product
                else:
                    acc_vmem[:, first:end] = product

    project((0, 1), ((wq_vmem, 0, q_cols),))

    def position_row(which):
        lines = [positions_ref[pl.ds(which * (tokens // W) + i, 1), :] for i in range(tokens // W)]
        return jnp.concatenate(lines, axis=1)

    my_positions = position_row(ctx)
    spread = jnp.broadcast_to(my_positions, (tokens, tokens))
    diagonal = lax.broadcasted_iota(jnp.int32, (tokens, tokens), 0) == lax.broadcasted_iota(
        jnp.int32, (tokens, tokens), 1
    )
    column = jnp.sum(jnp.where(diagonal, spread, 0).astype(F32), axis=1, keepdims=True)
    thousands = jnp.floor((column + (scale_base + 1.0)) * (1.0 / 8192.0))
    scaling = (jnp.log(thousands + 1.0) * 0.1 + 1.0) / math.sqrt(W)
    q_vmem[:tokens, :] = (acc_vmem[:, :q_cols] * scaling).astype(BF16)
    rows_own, rows_peer = pl.ds(0, tokens), pl.ds(tokens, tokens)
    ask = send(q_vmem.at[rows_own], q_vmem.at[rows_peer], (y_peer, head))
    project((2, 3), ((wk_vmem, q_cols, q_cols + W), (wv_vmem, q_cols + W, q_cols + 2 * W)))
    new_vmem[...] = acc_vmem[:, q_cols:].astype(BF16)
    fresh = [
        send(new_vmem, all_new.at[last], (right, head)),
        send(new_vmem, all_new.at[2], (left, head)),
        send(new_vmem, all_new.at[4], (far, head)),
    ]
    fresh_pair = [send(new_vmem, all_new.at[1], (sibling, head))]
    all_new[0] = new_vmem[...]
    for i in range(1, PIECES):
        send_near(i)
    send_slabs(1)

    def positions_of(which):
        return position_row(which).astype(F32)

    def as_column(row):
        spread = jnp.where(diagonal, jnp.broadcast_to(row, (tokens, tokens)), 0.0)
        return jnp.sum(spread, axis=1, keepdims=True)

    mine = jnp.concatenate([column, as_column(positions_of(y_peer))], axis=0)
    for slot in range(2 * x_count):
        theirs = positions_of(at(dx=slot // 2, dc=slot % 2))
        bias_ref[slot // 4, :, (slot % 4) * tokens : (slot % 4 + 1) * tokens] = jnp.where(
            theirs > mine, MASKED, 0.0
        )

    for copy, everyone, held, sem in zip(pair[:2], (all_keys, all_values), (near_k, near_v), (7, 8)):
        copy.wait_recv()
        load = pltpu.make_async_copy(everyone.at[1], held.at[pl.ds(keep, keep)], local_sem.at[sem])
        load.start()
        near_loads.append(load)
    for load in near_loads:
        load.wait()
    own = [
        pltpu.make_async_copy(held.at[pl.ds(0, keep)], everyone.at[0], local_sem.at[i])
        for i, (held, everyone) in enumerate(((near_k, all_keys), (near_v, all_values)))
    ]
    for copy in own:
        copy.start()

    near_args = (list_ref, 0, 0, NEAR, list_ref[3 * LIST], near_k, near_v)

    def new_block(b):
        pieces = [all_new[4 * b + j] for j in range(4)]
        block = jnp.concatenate(pieces, axis=0)
        return block[:, :W], block[:, W:], lambda: bias_ref[b]

    def peaks_of(rows):
        here = slice(rows * tokens, (rows + 1) * tokens)
        keys, _, row = some_pages(*near_args)
        for g in range(G):
            s = score(q_vmem, g, keys, lambda: row, here)
            m_ref[g, here] = jnp.maximum(
                jnp.max(s, axis=1, keepdims=True), jnp.full((tokens, W), LOW, F32)
            )
        if rows == 0:
            for copy, slot in zip(fresh, (last, 2, 4)):
                copy.wait_recv()
                fresh_pair.append(send(all_new.at[slot], all_new.at[slot + 1], (sibling, head)))
            for copy in fresh_pair:
                copy.wait_recv()

        def new_peak(b, _):
            keys, _, _ = new_block(b)
            for g in range(G):
                s = score(q_vmem, g, keys, lambda: bias_ref[b, here], here)
                m_ref[g, here] = jnp.maximum(m_ref[g, here], jnp.max(s, axis=1, keepdims=True))
            return 0

        lax.fori_loop(0, x_count // 2, new_peak, 0)

    peaks_of(0)
    send_slabs(2)
    ask.wait_recv()
    late = [pltpu.make_async_copy(q_vmem, queries, local_sem.at[3])]
    late[0].start()
    peaks_of(1)
    lane = lax.broadcasted_iota(jnp.int32, (2 * tokens, W), 1)
    stats = jnp.zeros((2 * tokens, W), F32)
    for g in range(G):
        stats = jnp.where(lane == g, m_ref[g], stats)
    stats_out[...] = stats.T[:8]
    peaks = send(stats_out, stats_in, (y_peer, head))

    across, near_pair, side_loads = [], [], []

    def pass_on(i):
        for which, (_, everyone) in enumerate(both):
            for slot in (last, 2):
                near[which, slot, i].wait_recv()
                here = everyone.at[slot, thirds[i]]
                if which == 0 and slot == last:
                    across.append(send(here, everyone.at[4, thirds[i]], (right, head)))
                if which == 1 and slot == 2:
                    across.append(send(here, everyone.at[4, thirds[i]], (left, head)))
                near_pair.append(send(here, everyone.at[slot + 1, thirds[i]], (sibling, head)))

    pass_on(0)
    peaks.wait_recv()
    their_peaks = jnp.concatenate([stats_in[...]] * (W // 8), axis=0).T
    for g in range(G):
        theirs = their_peaks[:, g : g + 1]
        theirs = jnp.concatenate([theirs[tokens:], theirs[:tokens]], axis=0)
        m_ref[g] = jnp.maximum(m_ref[g], theirs)

    keys, values, row = some_pages(*near_args)
    for g in range(G):
        l_ref[g], acc_ref[g] = weigh(score(q_vmem, g, keys, lambda: row), wide(m_ref[g], keys), values)

    for i in range(1, PIECES):
        pass_on(i)
    send_slabs(len(out_peers))

    def hold(odd):
        for which, (_, everyone) in enumerate(both):
            for spot, slot in ((0, 2), (2, last)):
                load = pltpu.make_async_copy(
                    everyone.at[slot + odd],
                    (side_k, side_v)[which].at[pl.ds((spot + odd) * keep, keep)],
                    local_sem.at[9 + len(side_loads)],
                )
                load.start()
                side_loads.append(load)

    hold(0)

    def new_weights(b, _):
        keys, values, bias = new_block(b)
        for g in range(G):
            sums, summed = weigh(score(q_vmem, g, keys, bias), wide(m_ref[g], keys), values)
            l_ref[g] += sums
            acc_ref[g] += summed
        return 0

    lax.fori_loop(0, x_count // 2, new_weights, 0)

    for copy in near_pair:
        copy.wait_recv()
    hold(1)
    for load in side_loads:
        load.wait()
    keys, values, row = some_pages(list_ref, 1, 0, SIDE, list_ref[3 * LIST + 1], side_k, side_v)
    for g in range(G):
        absorb(q_vmem, g, keys, values, lambda: row, acc_ref, m_ref, l_ref)

    across_pair = []
    for i, copy in enumerate(across):
        copy.wait_recv()
        everyone, here = both[i % 2][1], thirds[i // 2]
        across_pair.append(send(everyone.at[4, here], everyone.at[5, here], (sibling, head)))
    for copy in slabs:
        copy.wait_recv()
    for copy in across_pair:
        copy.wait_recv()
    for copy in list(near.values()) + pair + fresh + fresh_pair + across + near_pair + across_pair:
        copy.wait_send()
    for copy in [ask, peaks]:
        copy.wait_send()
    for copy in slabs:
        copy.wait_send()
    for copy in own + late:
        copy.wait()


def gather(lists, positions, hidden, w_query, w_key, w_value, w_out, keys, values, x_count, z_count):
    held = keys.shape[0]
    tokens, depth = hidden.shape
    q_cols = w_query.shape[1]
    columns = w_out.shape[1] // (2 * z_count)
    anywhere = pl.BlockSpec(memory_space=pl.ANY)
    vmem = pl.BlockSpec(memory_space=pltpu.VMEM)
    steps = 5
    copies = 64
    state = jax.ShapeDtypeStruct((G, 2 * tokens, W), F32)
    return pl.pallas_call(
        functools.partial(gather_kernel, x_count, z_count, float(held * PAGE * x_count * 4)),
        out_shape=[
            jax.ShapeDtypeStruct((2 * x_count, held, PAGE, W), BF16),
            jax.ShapeDtypeStruct((2 * x_count, held, PAGE, W), BF16),
            jax.ShapeDtypeStruct((2 * tokens, q_cols), BF16),
            jax.ShapeDtypeStruct((2 * z_count, w_out.shape[0], columns), BF16),
            state,
            state,
            state,
        ],
        in_specs=[pl.BlockSpec(memory_space=pltpu.SMEM), vmem] + [anywhere] * 7,
        out_specs=[anywhere] * 4 + [vmem] * 3,
        scratch_shapes=[
            pltpu.VMEM((tokens, depth), BF16),
            pltpu.VMEM((depth, q_cols), BF16),
            pltpu.VMEM((depth, W), BF16),
            pltpu.VMEM((depth, W), BF16),
            pltpu.VMEM((tokens, q_cols + 2 * W), F32),
            pltpu.VMEM((2 * tokens, q_cols), BF16),
            pltpu.VMEM((tokens, 2 * W), BF16),
            pltpu.VMEM((2 * x_count, tokens, 2 * W), BF16),
            pltpu.VMEM((2 * held, PAGE, W), BF16),
            pltpu.VMEM((2 * held, PAGE, W), BF16),
            pltpu.VMEM((4 * held, PAGE, W), BF16),
            pltpu.VMEM((4 * held, PAGE, W), BF16),
            pltpu.VMEM((x_count // 2, 2 * tokens, 4 * tokens), F32),
            pltpu.VMEM((8, 2 * tokens), F32),
            pltpu.VMEM((8, 2 * tokens), F32),
            pltpu.SemaphoreType.DMA((copies,)),
            pltpu.SemaphoreType.DMA((copies,)),
            pltpu.SemaphoreType.DMA((steps, 4)),
            pltpu.SemaphoreType.DMA((17,)),
        ],
        compiler_params=pltpu.CompilerParams(
            collective_id=0, has_side_effects=True, vmem_limit_bytes=60 * 2**20
        ),
    )(lists, positions, hidden, w_query, w_key, w_value, w_out, keys, values)


def extra_kernel(
    list_ref, q_any, k_any, v_any, acc_in, m_in, l_in, acc_any, m_any, l_any, q, k, v, acc, m, l, sem
):
    count = list_ref[3 * LIST + 2]

    @pl.when(count > REST)
    def _():
        pairs = [(q_any, q), (k_any, k), (v_any, v), (acc_any, acc), (m_any, m), (l_any, l)]
        copies = [pltpu.make_async_copy(a, b, sem.at[i]) for i, (a, b) in enumerate(pairs)]
        for copy in copies:
            copy.start()
        for copy in copies:
            copy.wait()

        def step(i, _):
            keys, values, row = some_pages(list_ref, 2, REST + i * 4, 4, count, k, v)
            for g in range(G):
                absorb(q, g, keys, values, lambda: row, acc, m, l)
            return 0

        lax.fori_loop(0, (count - REST + 3) // 4, step, 0)
        back = [pltpu.make_async_copy(b, a, sem.at[i]) for i, (a, b) in enumerate(pairs[3:])]
        for copy in back:
            copy.start()
        for copy in back:
            copy.wait()


def extra(lists, queries, keys, values, acc, m, l):
    anywhere = pl.BlockSpec(memory_space=pl.ANY)
    state = jax.ShapeDtypeStruct(acc.shape, F32)
    return pl.pallas_call(
        extra_kernel,
        out_shape=[state] * 3,
        in_specs=[pl.BlockSpec(memory_space=pltpu.SMEM)] + [anywhere] * 6,
        out_specs=[anywhere] * 3,
        input_output_aliases={4: 0, 5: 1, 6: 2},
        scratch_shapes=[
            pltpu.VMEM(queries.shape, BF16),
            pltpu.VMEM(keys.shape, BF16),
            pltpu.VMEM(values.shape, BF16),
            pltpu.VMEM(acc.shape, F32),
            pltpu.VMEM(acc.shape, F32),
            pltpu.VMEM(acc.shape, F32),
            pltpu.SemaphoreType.DMA((6,)),
        ],
        compiler_params=pltpu.CompilerParams(vmem_limit_bytes=60 * 2**20),
    )(lists, queries, keys, values, acc, m, l)


def finish_kernel(
    x_count,
    z_count,
    list_ref,
    q_any,
    k_any,
    v_any,
    acc_any,
    m_any,
    l_any,
    w_out_ref,
    slab_ref,
    out_ref,
    q_ref,
    k_ref,
    v_ref,
    acc_ref,
    m_ref,
    l_ref,
    acc_in,
    stats_out,
    stats_in,
    slab_vmem,
    heads,
    send_sem,
    recv_sem,
    load_sem,
):
    ctx, head, core, at = places(x_count)
    z, y_lo = head // 2, head % 2
    tokens = acc_in.shape[1]
    y_peer = at(dy=1)

    def head_at(dz, dl):
        return lax.rem(z + dz, z_count) * 2 + lax.rem(y_lo + dl, 2)

    above, below, beside = head_at(1, 0), head_at(z_count - 1, 0), head_at(0, 1)
    loads = [
        pltpu.make_async_copy(source, target, load_sem.at[i])
        for i, (source, target) in enumerate(
            [
                (q_any, q_ref),
                (k_any, k_ref),
                (v_any, v_ref),
                (acc_any, acc_ref),
                (m_any, m_ref),
                (l_any, l_ref),
            ]
        )
    ]
    columns = slab_ref.shape[2]
    half = slab_ref.shape[1] // 2
    my_half = pl.ds(pl.multiple_of(core * half, half), half)
    my_cols = pl.ds(pl.multiple_of(head * columns, columns), columns)
    others = [lax.rem(head + i, 2 * z_count) for i in range(1, 2 * z_count)]
    weights = [pltpu.make_async_copy(w_out_ref.at[:, my_cols], slab_vmem.at[head], load_sem.at[6])]
    for i, which in enumerate(others):
        weights.append(
            pltpu.make_async_copy(
                slab_ref.at[which, my_half], slab_vmem.at[which, my_half], load_sem.at[7 + i]
            )
        )
    for load in loads + weights:
        load.start()

    barrier = pltpu.get_barrier_semaphore()
    met = [(y_peer, head), (at(dc=1), head), (ctx, above), (ctx, below), (ctx, beside)]
    for device in met:
        pl.semaphore_signal(barrier, inc=1, device_id=device, device_id_type=MESH)
    pl.semaphore_wait(barrier, len(met))

    counter = [0]
    started = []

    def send(source, target, device):
        i = counter[0]
        counter[0] += 1
        copy = pltpu.make_async_remote_copy(
            src_ref=source,
            dst_ref=target,
            send_sem=send_sem.at[i],
            recv_sem=recv_sem.at[i],
            device_id=device,
            device_id_type=MESH,
        )
        copy.start()
        started.append(copy)
        return copy

    halves = [
        send(slab_ref.at[which, my_half], slab_vmem.at[which, my_half], (at(dc=1), head))
        for which in others
    ]
    rows_peer = pl.ds(tokens, tokens)
    lane_row = lax.broadcasted_iota(jnp.int32, (tokens, W), 1)
    for load in loads:
        load.wait()
    blocks = [
        some_pages(list_ref, 2, first, BLOCK, list_ref[3 * LIST + 2], k_ref, v_ref)
        for first in range(0, REST, BLOCK)
    ]
    stats_copies, parts = [], []

    def attend(g):
        for keys, values, row in blocks:
            absorb(q_ref, g, keys, values, lambda: row, acc_ref, m_ref, l_ref)
        l_ref[g] = jnp.broadcast_to(jnp.sum(l_ref[g], axis=1, keepdims=True), l_ref.shape[1:])
        stats_out[g] = jnp.where(lane_row == 0, m_ref[g, tokens:], l_ref[g, tokens:]).T[:8]
        stats_copies.append(send(stats_out.at[g], stats_in.at[g], (y_peer, head)))
        parts.append(send(acc_ref.at[g, rows_peer], acc_in.at[g], (y_peer, head)))

    def pass_on(who, g, device):
        return send(heads.at[who, g], heads.at[who, g], (ctx, device))

    def use(pieces, start):
        lhs = jnp.concatenate([heads[who, g] for who, g in pieces], axis=1)
        rhs = jnp.concatenate(
            [slab_vmem[who, g * W : (g + 1) * W, :] for who, g in pieces], axis=0
        )
        product = jnp.dot(lhs, rhs, preferred_element_type=F32)
        if start:
            out_ref[...] = product
        else:
            out_ref[...] += product

    up, down, side, up_side, down_side, two, two_side = ({} for _ in range(7))
    attend(0)
    for t in range(G + 3):
        ready = []
        g = t
        if g + 1 < G:
            attend(g + 1)
        if g < G:
            stats_copies[g].wait_recv()
            parts[g].wait_recv()
            m1, l1 = m_ref[g, :tokens], l_ref[g, :tokens]
            theirs = jnp.concatenate([stats_in[g]] * (W // 8), axis=0).T
            m2, l2 = theirs[:, 0:1], theirs[:, 1:2]
            m = jnp.maximum(m1, m2)
            a1, a2 = jnp.exp(m1 - m), jnp.exp(m2 - m)
            total = l1 * a1 + l2 * a2
            heads[head, g] = (acc_ref[g, :tokens] * (a1 / total) + acc_in[g] * (a2 / total)).astype(BF16)
            side[g] = pass_on(head, g, beside)
            up[g] = pass_on(head, g, above)
            down[g] = pass_on(head, g, below)
            ready.append((head, g))
        g = t - 1
        if 0 <= g < G:
            side[g].wait_recv()
            up_side[g] = pass_on(beside, g, above)
            down_side[g] = pass_on(beside, g, below)
            up[g].wait_recv()
            down[g].wait_recv()
            if g % 2 == 0:
                two[g] = pass_on(below, g, above)
            else:
                two[g] = pass_on(above, g, below)
            ready += [(beside, g), (below, g), (above, g)]
        g = t - 2
        if 0 <= g < G:
            up_side[g].wait_recv()
            down_side[g].wait_recv()
            if g % 2 == 1:
                two_side[g] = pass_on(head_at(z_count - 1, 1), g, above)
            else:
                two_side[g] = pass_on(head_at(1, 1), g, below)
            ready += [(head_at(z_count - 1, 1), g), (head_at(1, 1), g)]
        g = t - 3
        if 0 <= g < G:
            two[g].wait_recv()
            two_side[g].wait_recv()
            ready += [(head_at(2, 0), g), (head_at(2, 1), g)]
        if t == 0:
            for load in weights:
                load.wait()
        if t == 1:
            for copy in halves:
                copy.wait_recv()
        use(ready, t == 0)
    for copy in started:
        copy.wait_send()


def finish(lists, queries, keys, values, acc, m, l, w_out, slab, x_count, z_count):
    tokens = queries.shape[0] // 2
    anywhere = pl.BlockSpec(memory_space=pl.ANY)
    copies = G * 9 + 2 * z_count
    return pl.pallas_call(
        functools.partial(finish_kernel, x_count, z_count),
        out_shape=jax.ShapeDtypeStruct((tokens, slab.shape[2]), F32),
        in_specs=[pl.BlockSpec(memory_space=pltpu.SMEM)] + [anywhere] * 8,
        out_specs=pl.BlockSpec(memory_space=pltpu.VMEM),
        scratch_shapes=[
            pltpu.VMEM(queries.shape, BF16),
            pltpu.VMEM(keys.shape, BF16),
            pltpu.VMEM(values.shape, BF16),
            pltpu.VMEM(acc.shape, F32),
            pltpu.VMEM(acc.shape, F32),
            pltpu.VMEM(acc.shape, F32),
            pltpu.VMEM((G, tokens, W), F32),
            pltpu.VMEM((G, 8, tokens), F32),
            pltpu.VMEM((G, 8, tokens), F32),
            pltpu.VMEM(slab.shape, BF16),
            pltpu.VMEM((2 * z_count, G, tokens, W), BF16),
            pltpu.SemaphoreType.DMA((copies,)),
            pltpu.SemaphoreType.DMA((copies,)),
            pltpu.SemaphoreType.DMA((6 + 2 * z_count,)),
        ],
        compiler_params=pltpu.CompilerParams(
            collective_id=1, has_side_effects=True, vmem_limit_bytes=60 * 2**20
        ),
    )(lists, queries, keys, values, acc, m, l, w_out, slab)


def on_device(
    hidden,
    positions,
    w_query,
    key_matrix,
    value_matrix,
    w_out,
    stored_keys,
    stored_values,
    kept_pages,
    page_slot,
):
    tokens = hidden.shape[0]
    ctx_count, head_count = lax.axis_size("ctx"), lax.axis_size("head")
    x_count, z_count = ctx_count // 4, head_count // 2
    table = positions.reshape(-1, W)
    lists = page_lists(kept_pages, page_slot, x_count)
    keys, values, queries, slab, acc, m, l = gather(
        lists, table, hidden, w_query, key_matrix, value_matrix, w_out,
        stored_keys.reshape(-1, PAGE, W), stored_values.reshape(-1, PAGE, W),
        x_count, z_count,
    )
    keys, values = keys.reshape(-1, PAGE, W), values.reshape(-1, PAGE, W)
    acc, m, l = extra(lists, queries, keys, values, acc, m, l)
    return finish(lists, queries, keys, values, acc, m, l, w_out, slab, x_count, z_count)


def solution(mesh):
    placed = (
        P("ctx", None),
        P(),
        P(None, "head"),
        P(None, "head"),
        P(None, "head"),
        P("head", None),
        P("ctx", "head"),
        P("ctx", "head"),
        P(),
        P(),
    )
    return jax.shard_map(
        on_device, mesh=mesh, in_specs=placed, out_specs=P("ctx", "head"), check_vma=False
    )
```
